32 devices in a mesh: stream: 4 (over z), mod: 8 (over y, x, core).
Axes of the slice: x: 2, y: 2, z: 4, core: 2. Of those that a mesh axis runs over, the one named last changes fastest.
Arguments:
- pixels: bfloat16 [4, 192, 128, 384], P('stream', None, 'mod'), may hold values from -6 to 6
- stem_weight: bfloat16 [256, 128], replicated, may hold values from -0.375 to 0.375
- veto_weight: float32 [8, 128], replicated, may hold values from -0.25 to 0.25
- hit_frames: int32 [4, 48], P('stream'), may hold values from 0 to 191, as said below
- assign: int32 [4, 48, 1], P('stream'), may hold values from 0 to 3; in each aligned block of 6 rows (0 to 5, 6 to 11, ..., all dimensions but the last counted through in order) at most 2 rows name the same one
- token_in: bfloat16 [4, 384, 24], P('stream'), may hold values from -1.25 to 1.25
- token_out: bfloat16 [4, 24, 384], P('stream'), may hold values from -0.3125 to 0.3125
- chan_in: bfloat16 [4, 128, 512], P('stream'), may hold values from -0.5 to 0.5
- chan_out: bfloat16 [4, 512, 128], P('stream'), may hold values from -0.25 to 0.25
- readout: bfloat16 [1024, 128], replicated, may hold values from -0.1875 to 0.1875
- latent_gain: float32 [128], replicated, may hold values from 0.1 to 1.9
- class_weight: float32 [128, 8], replicated, may hold values from -0.5 to 0.5
Outputs:
- veto: float32 [4, 192], P('stream', 'mod')
- latents: float32 [4, 48, 128], P('stream', 'mod')
- scores: float32 [4, 48, 8], P('stream', 'mod')
The draws below stay inside these ranges and needn't reach their ends.
Inputs may be any that keep to these rules, and one draw needn't show every extreme that they name: `hit_frames`: each row lists, rising and distinct, exactly 6 frames from every aligned block of 24 frames. `assign`: within the 6 hits of one aligned block (one owner's hits) no stream is named more than 2 times.
All inputs are finite; a program needn't handle non-finite values.
Results may differ from the reference program's by a relative error of at most 0.0095.
Values may be sent and summed in bfloat16 or wider, within the bound.
No kernel may reach another device: no remote copies, remote signals or barrier semaphores. Data moves between devices by JAX's collectives and lax.ppermute only.
A program may use at most 128 MiB of HBM per device.

```python
import math
import jax
import jax.numpy as jnp
import numpy as np
from jax import lax

C = 128
TMIX = 384
HID = 512
NCLS = 8
PATCH = 16
ROWS_DEV = 16
COLS = 384
FR_DEV = 24
CAP = 2
WT = 24
FRAMES = 192
HIT_DEV = 6
HITS = 48
N_STREAM = 4
N_MOD = 8


def draw_hit_frames(key, part):
    owners = FRAMES // FR_DEV
    n_blocks = N_STREAM * owners
    random_keys = jax.random.randint(key, (n_blocks, FR_DEV), 0, 2 ** 20)
    distinct = random_keys * FR_DEV + jnp.arange(FR_DEV, dtype=jnp.int32)[None, :]
    picked = jnp.sort(jnp.argsort(distinct, axis=1)[:, :HIT_DEV].astype(jnp.int32), axis=1)
    offsets = jnp.arange(n_blocks, dtype=jnp.int32) % owners * FR_DEV
    return (picked + offsets[:, None]).astype(jnp.int32).reshape(N_STREAM, HITS)


def steps_of(key, extent, shards, smallest, largest):
    loudness, own = 1.0, jax.random.fold_in(key, 6)
    for axis_at, blocks in shards:
        steps = jnp.exp(jax.random.uniform(jax.random.fold_in(own, axis_at), (blocks,), jnp.float32, smallest / len(shards), largest / len(shards)))
        loudness = loudness * jnp.repeat(steps, extent[axis_at] // blocks).reshape([-1 if axis == axis_at else 1 for axis in range(len(extent))])
    return loudness


def routed_block(rng, own, number, rows, count, top, limit, slope):
    sequence = jax.random.permutation(rng, count)
    crowded, common = load_shares(count, rows * top, limit, slope, True), load_shares(count, rows * top, limit, slope, False)
    places = jnp.arange(count)

    def named(sizes, turn):
        used = int((sizes > 0).sum())
        fixed = max(1, used // 4)
        shifted = fixed + (places - fixed + turn * (used - fixed)) % max(1, count - fixed)
        return jnp.zeros((count,), jnp.int32).at[sequence[jnp.where(places < fixed, places, shifted)]].set(jnp.asarray(sizes, jnp.int32))

    sizes = jnp.where(number % 4 == 0, named(crowded, number // 4), named(common, number - number // 4 - 1))
    mixed = jax.random.permutation(jax.random.fold_in(own, 3), count)
    donor, sink = mixed[0:count // 2 * 2:2], mixed[1:count // 2 * 2:2]
    slack = jnp.minimum(sizes[donor] - 1, limit - sizes[sink]) // 2
    slack = jnp.where((donor == sequence[0]) | (sink == sequence[0]) | (sizes[sink] == 0), 0, jnp.maximum(slack, 0))
    shifted = jax.random.randint(jax.random.fold_in(own, 4), (count // 2,), 0, 1 << 20) % (slack + 1)
    sizes = sizes.at[donor].add(-shifted).at[sink].add(shifted)
    members = jnp.searchsorted(jnp.cumsum(sizes), jnp.arange(rows * top), side="right").astype(jnp.int32)
    grid = members.reshape(top, rows).T
    grid = grid[jax.random.permutation(jax.random.fold_in(own, 1), rows)]
    turn = jax.random.randint(jax.random.fold_in(own, 2), (rows, 1), 0, top)
    return jnp.take_along_axis(grid, (jnp.arange(top)[None, :] + turn) % top, axis=1)


def load_shares(count, total, reach, slope, full):
    portions = [(1 << 20) // math.isqrt(standing ** slope) + 1 for standing in range(1, count + 1)]
    largest = reach if full else min(reach, max(-(-total // count), total * portions[0] // sum(portions)))
    least = 1 if total - largest >= count - 1 else 0
    holding, surplus = [largest] + [least] * (count - 1), total - largest - least * (count - 1)
    while surplus > 0:
        free = [i for i in range(1, count) if holding[i] < largest] or [i for i in range(1, count) if holding[i] < reach]
        whole, budget = sum([portions[i] for i in free]), surplus
        for i in free:
            extra = min(reach - holding[i], max(1, budget * portions[i] // whole), surplus)
            holding[i] = holding[i] + extra
            surplus = surplus - extra
    return np.array(holding)


def bell_draw(own_key, shape, spread, limit, shards=(), kind=jnp.bfloat16):
    entries = spread * jax.random.normal(own_key, shape, jnp.float32)
    if shards:
        entries = entries * steps_of(own_key, shape, shards, -0.22, 0.18)
    return jnp.clip(entries, -limit, limit).astype(kind)


def setup_inputs(seed: int = 0) -> dict:
    arg_keys = jax.random.split(jax.random.key(seed), 13)
    pixels = bell_draw(arg_keys[0], (N_STREAM, FRAMES, N_MOD * ROWS_DEV, COLS), 1.0, 6.0, ((0, 4), (2, 8)))
    stem_weight = bell_draw(arg_keys[1], (PATCH * PATCH, C), (PATCH * PATCH) ** -0.5, 0.375)
    veto_weight = bell_draw(arg_keys[2], (N_MOD, C), (4 * C) ** -0.5, 0.25, (), jnp.float32)
    hit_frames = draw_hit_frames(jax.random.fold_in(arg_keys[12], 71), 0)
    assign_keys = jax.random.split(jax.random.fold_in(arg_keys[4], 1), N_STREAM * HITS // HIT_DEV)
    assign_turns = jax.random.permutation(jax.random.fold_in(arg_keys[4], 3), N_STREAM * HITS // HIT_DEV)
    assign = jax.vmap(lambda own, number: routed_block(jax.random.fold_in(arg_keys[4], 2), own, number, HIT_DEV, N_STREAM, 1, CAP, 2))(assign_keys, assign_turns).reshape((N_STREAM, HITS, 1))
    token_in = bell_draw(arg_keys[5], (N_STREAM, TMIX, WT), WT ** -0.5, 1.25, ((0, 4),))
    token_out = bell_draw(arg_keys[6], (N_STREAM, WT, TMIX), TMIX ** -0.5, 0.3125, ((0, 4),))
    chan_in = bell_draw(arg_keys[7], (N_STREAM, C, HID), C ** -0.5, 0.5, ((0, 4),))
    chan_out = bell_draw(arg_keys[8], (N_STREAM, HID, C), HID ** -0.5, 0.25, ((0, 4),))
    readout = bell_draw(arg_keys[9], (N_MOD * C, C), (N_MOD * C) ** -0.5, 0.1875)
    latent_gain = jnp.clip(1.0 + 0.18 * jax.random.normal(arg_keys[10], (C,), jnp.float32), 0.1, 1.9)
    class_weight = bell_draw(arg_keys[11], (C, NCLS), C ** -0.5, 0.5, (), jnp.float32)
    return {"pixels": pixels, "stem_weight": stem_weight, "veto_weight": veto_weight, "hit_frames": hit_frames, "assign": assign, "token_in": token_in, "token_out": token_out, "chan_in": chan_in, "chan_out": chan_out, "readout": readout, "latent_gain": latent_gain, "class_weight": class_weight}


def rms_norm(values):
    return values * lax.rsqrt(lax.optimization_barrier(jnp.mean(values * values, axis=-1, keepdims=True)) + 1e-06)

def stem_layer(frame_pixels, stem_weight):
    count, height, width = frame_pixels.shape
    pixel_tiles = frame_pixels.astype(jnp.float32).reshape(count, height // PATCH, PATCH, width // PATCH, PATCH)
    kernel = stem_weight.astype(jnp.float32).reshape(PATCH, PATCH, -1)
    response = jnp.einsum('fapbq,pqc->fabc', pixel_tiles, kernel)
    return jax.nn.gelu(response).astype(jnp.bfloat16).reshape(count, -1, kernel.shape[-1])

def encode(tokens, mix_in, mix_out, chan_in, chan_out, readout, latent_gain, class_weight):
    batch = tokens.shape[0]
    channels = tokens.shape[-1]
    row_len = mix_in.shape[1]
    resid = tokens.astype(jnp.float32).reshape(batch, -1, row_len, channels)
    normed = rms_norm(resid).astype(jnp.bfloat16)
    mixed_tok = jax.nn.gelu(jnp.einsum('mw,brwc->brmc', mix_in.astype(jnp.float32), normed.astype(jnp.float32))).astype(jnp.bfloat16)
    after_mix = (resid + jnp.einsum('wm,brmc->brwc', mix_out.astype(jnp.float32), mixed_tok.astype(jnp.float32))).astype(jnp.bfloat16)
    mix_float = after_mix.astype(jnp.float32).reshape(batch, -1, channels)
    normed_two = rms_norm(mix_float).astype(jnp.bfloat16)
    hidden = jax.nn.gelu(jnp.einsum('btc,ch->bth', normed_two.astype(jnp.float32), chan_in.astype(jnp.float32))).astype(jnp.bfloat16)
    after_mlp = mix_float + jnp.einsum('bth,hc->btc', hidden.astype(jnp.float32), chan_out.astype(jnp.float32))
    pooled = lax.optimization_barrier(jnp.mean(after_mlp.reshape(batch, N_MOD, -1, channels), axis=2)).reshape(batch, -1).astype(jnp.bfloat16)
    projected = jnp.dot(pooled, readout, preferred_element_type=jnp.float32)
    latent = rms_norm(projected) * latent_gain
    class_scores = jnp.dot(latent, class_weight, precision=lax.Precision.HIGHEST)
    return (latent, class_scores)

def reference(pixels, stem_weight, veto_weight, hit_frames, assign, token_in, token_out, chan_in, chan_out, readout, latent_gain, class_weight):
    veto_rows = []
    latent_rows = []
    score_rows = []
    for stream_id in range(N_STREAM):
        features = stem_layer(pixels[stream_id], stem_weight)
        module_means = lax.optimization_barrier(jnp.mean(features.astype(jnp.float32).reshape(FRAMES, N_MOD, -1, C), axis=2))
        veto_rows.append(lax.optimization_barrier(jnp.sum(module_means * veto_weight, axis=(1, 2))))
        chosen = jnp.take(features, hit_frames[stream_id].astype(jnp.int32), axis=0)
        targets = assign[stream_id, :, 0].astype(jnp.int32)

        def encode_hit(payload):
            frame_tokens, target = payload
            latent, class_scores = encode(frame_tokens[None], token_in[target], token_out[target], chan_in[target], chan_out[target], readout, latent_gain, class_weight)
            return (latent[0], class_scores[0])
        hit_latents, hit_scores = lax.map(encode_hit, (chosen, targets))
        latent_rows.append(hit_latents)
        score_rows.append(hit_scores)
    return (jnp.stack(veto_rows), jnp.stack(latent_rows), jnp.stack(score_rows))
```

```python
import functools
import math

import jax
import jax.numpy as jnp
from jax import lax
from jax.experimental import pallas as pl
from jax.experimental.pallas import tpu as pltpu
from jax.sharding import PartitionSpec as P

PATCH = 16
LANES = 128
GROUP = 16
VETO_ROWS = 16
PAD_ROW = 32
VMEM_BYTES = 60 * 1024 * 1024
ENCODE_VMEM_BYTES = 32 * 1024 * 1024
F32 = jnp.float32
BF16 = jnp.bfloat16
GELU_A = math.sqrt(2.0 / math.pi)
GELU_B = GELU_A * 0.044715


def gelu(x):
    half = 0.5 * x
    return half + half * jnp.tanh(x * (GELU_A + GELU_B * (x * x)))


def rms_norm(values):
    return values * lax.rsqrt(jnp.mean(values * values, axis=-1, keepdims=True) + 1e-06)


def dot(a, b):
    return jnp.dot(a, b, preferred_element_type=F32)


def iota(shape, axis):
    return lax.broadcasted_iota(jnp.int32, shape, axis)


def pack_kernel(token_in, token_out, chan_in, chan_out, mine, other, token_in_rows, token_out_rows, sems):
    core = lax.axis_index("mod") % 2
    channels, hidden = chan_in.shape
    width, mix = token_in.shape
    small = (
        pltpu.make_async_copy(token_in, token_in_rows, sems.at[0]),
        pltpu.make_async_copy(token_out, token_out_rows, sems.at[1]),
    )
    for c in small:
        c.start()

    def pack(first, second):
        large = [pltpu.make_async_copy(chan_out, second.at[pl.ds(0, hidden)], sems.at[2])]
        for j in range(hidden // LANES):
            large.append(
                pltpu.make_async_copy(
                    chan_in.at[:, pl.ds(j * LANES, LANES)], first.at[pl.ds(j * channels, channels)], sems.at[3 + j]
                )
            )
        for c in large:
            c.start()
        for c in small:
            c.wait()
        for source, ref in ((token_in_rows, first), (token_out_rows, second)):
            wide = source[...].astype(F32)
            wide = jnp.concatenate([wide, jnp.zeros((PAD_ROW - width, mix), F32)], axis=0).astype(BF16)
            for j in range(mix // LANES):
                ref[hidden + j * PAD_ROW : hidden + (j + 1) * PAD_ROW, :] = wide[:, j * LANES : (j + 1) * LANES]
        for c in large:
            c.wait()

    @pl.when(core == 0)
    def _():
        pack(mine, other)

    @pl.when(core == 1)
    def _():
        pack(other, mine)


def turn(tiles, span):
    count = len(tiles)
    lane = iota(tiles[0].shape, 1)
    size = span * count // 2
    half = count // 2
    while half:
        low = (lane // size) % 2 == 0
        done = list(tiles)
        for i in range(count):
            if i // half % 2 == 0:
                a, b = tiles[i], tiles[i + half]
                done[i] = jnp.where(low, a, roll(b, size))
                done[i + half] = jnp.where(low, roll(a, LANES - size), b)
        tiles, half, size = done, half // 2, size // 2
    return tiles


def roll(x, shift):
    return jnp.concatenate([x[:, LANES - shift :], x[:, : LANES - shift]], axis=1)


def stem_kernel(pixels, weight, veto_weight, hit_frames, out, images, rows, small, wide, veto_rows, hit_row, chosen, sems):
    frames, _, columns = images.shape
    owners = out.shape[0]
    hits = hit_frames.shape[1]
    owned = frames // owners
    hit_rows = out.shape[1] - VETO_ROWS
    channels = weight.shape[1]
    blocks = columns // LANES
    quads = LANES // (2 * PATCH)
    tokens = columns // PATCH
    pieces = sems.shape[0] - 3
    step = frames // pieces

    def copy(i):
        span = pl.ds(i * step, step)
        return pltpu.make_async_copy(pixels.at[span], images.at[span], sems.at[i])

    side = [
        pltpu.make_async_copy(weight, small, sems.at[pieces]),
        pltpu.make_async_copy(veto_weight, veto_rows, sems.at[pieces + 1]),
        pltpu.make_async_copy(hit_frames, hit_row, sems.at[pieces + 2]),
    ]
    for c in side:
        c.start()
    for i in range(pieces):
        copy(i).start()
    size = GROUP * PATCH
    r, c = iota((size, size), 0), iota((size, size), 1)
    swap = (c == (r % GROUP) * PATCH + r // GROUP).astype(F32).astype(BF16)
    for c in side:
        c.wait()
    zero = jnp.zeros((PATCH, channels), BF16)
    for p in range(PATCH):
        tile = small[p * PATCH : (p + 1) * PATCH, :]
        for a in range(2):
            top = (p * 2 + a) * PATCH
            for b in range(2):
                wide[top : top + PATCH, b * channels : (b + 1) * channels] = tile if a == b else zero
    for i in range(pieces):
        copy(i).wait()
        for g in range(i * step // GROUP, (i + 1) * step // GROUP):
            block = images[g * GROUP : (g + 1) * GROUP].reshape(size, columns)
            turned = dot(swap, block).astype(BF16)
            for j in range(blocks):
                for p in range(0, PATCH, quads):
                    tiles = [
                        turned[q * GROUP : (q + 1) * GROUP, j * LANES : (j + 1) * LANES] for q in range(p, p + quads)
                    ]
                    for n, tile in enumerate(turn(tiles, 2 * PATCH)):
                        top = (n * blocks + j) * frames + g * GROUP
                        rows[top : top + GROUP, p * 2 * PATCH : p * 2 * PATCH + LANES] = tile
    pick = (iota((frames, hits), 0) == hit_row[...]).astype(F32).T.astype(BF16)
    sums = jnp.zeros((frames, channels), F32)
    for n in range(quads):
        for j in range(blocks):
            top = (n * blocks + j) * frames
            part = gelu(dot(rows[top : top + frames, :], wide[...]))
            sums = sums + part[:, :channels] + part[:, channels:]
            taken = dot(pick, part.astype(BF16))
            for k in range(2):
                chosen[pl.ds(j * 2 * quads + 2 * n + k, hits, stride=tokens), :] = taken[
                    :, k * channels : (k + 1) * channels
                ]
    scale = jnp.broadcast_to(veto_rows[pl.ds(lax.axis_index("mod"), 1), :] / tokens, (VETO_ROWS, channels))
    row = iota((VETO_ROWS, owned), 0)
    for o in range(owners):
        out[o, 0:hit_rows, :] = chosen[o * hit_rows : (o + 1) * hit_rows, :].astype(BF16)
        veto = lax.dot_general(
            scale,
            sums[o * owned : (o + 1) * owned],
            (((1,), (1,)), ((), ())),
            preferred_element_type=F32,
            precision=lax.Precision.HIGHEST,
        )
        high = veto.astype(BF16).astype(F32)
        both = jnp.where(row == 0, high, jnp.where(row == 1, veto - high, 0.0))
        both = jnp.concatenate([both, jnp.zeros((VETO_ROWS, LANES - owned), F32)], axis=1)
        out[o, hit_rows : hit_rows + VETO_ROWS, :] = both.astype(BF16)


def encode_kernel(streams, width, hidden, *refs):
    features, targets, readout, gain, class_weight = refs[:5]
    halves = refs[5 : 5 + 2 * streams]
    veto, latents, scores, table, pools, sems = refs[5 + 2 * streams :]
    owners = features.shape[0]
    channels = features.shape[2]
    hits = latents.shape[0]
    hit_rows = hits * width
    here = lax.axis_index("stream")
    own = lax.axis_index("mod")
    core = own % 2
    copies = []
    for k in range(streams):
        copies.append(pltpu.make_async_copy(halves[2 * k], table.at[k, core], sems.at[2 * k]))
        copies.append(pltpu.make_async_copy(halves[2 * k + 1], table.at[k, 1 - core], sems.at[2 * k + 1]))
    for c in copies:
        c.start()
    terms = jnp.sum(features[:, hit_rows : hit_rows + VETO_ROWS, :].astype(F32), axis=0)
    veto[...] = jnp.sum(terms, axis=0, keepdims=True)[:, : veto.shape[1]]
    pools[...] = jnp.zeros_like(pools)
    for c in copies:
        c.wait()

    def encode(slot, x):
        target = targets[own * hits + slot]
        k = target ^ here
        extra = table.shape[2] - hidden
        blocks = extra // PAD_ROW
        packed = table[k, 0, hidden:, :].astype(F32)
        token_in = jnp.concatenate([packed[j * PAD_ROW : (j + 1) * PAD_ROW] for j in range(blocks)], axis=1)
        token_in = token_in.T.astype(BF16)
        normed = rms_norm(x)
        gap = jnp.zeros((PAD_ROW - width, channels), F32)
        wide = jnp.concatenate(
            [jnp.concatenate([normed[r], gap], axis=0).astype(BF16) for r in range(owners)], axis=1
        )
        mixed = gelu(dot(token_in, wide)).astype(BF16)
        mix_rows = table[k, 1, hidden:, :]
        token_out = jnp.concatenate(
            [mix_rows[j * PAD_ROW : (j + 1) * PAD_ROW] for j in range(blocks)], axis=1
        )
        back = dot(token_out, mixed)
        after = jnp.concatenate(
            [x[r] + back[:width, r * channels : (r + 1) * channels] for r in range(owners)], axis=0
        )
        after = after.astype(BF16).astype(F32)
        chan_in = jnp.concatenate(
            [table[k, 0, j * channels : (j + 1) * channels, :] for j in range(hidden // channels)], axis=1
        )
        inner = gelu(dot(rms_norm(after).astype(BF16), chan_in)).astype(BF16)
        last = after + dot(inner, table[k, 1, 0:hidden, :])
        pool = jnp.sum(last.reshape(owners, width, channels), axis=1) * (1.0 / width)
        pools[pl.ds(pl.multiple_of(slot * owners, owners), owners), :] = pool

    pair = 2

    @pl.loop(0, hits // pair)
    def _(i):
        x = features[:, pl.ds(pl.multiple_of(i * pair * width, 16), pair * width), :].astype(F32)
        for a in range(pair):
            encode(i * pair + a, x[:, a * width : (a + 1) * width])

    pooled = jnp.concatenate(
        [pools[pl.ds(r, 8, stride=owners), :].astype(BF16) for r in range(owners)], axis=1
    )
    latent = rms_norm(dot(pooled, readout[...])) * gain[...]
    latents[:, 0, :] = latent[:hits]
    scores[:, 0, :] = lax.dot_general(
        latent,
        class_weight[...],
        (((1,), (1,)), ((), ())),
        preferred_element_type=F32,
        precision=lax.Precision.HIGHEST,
    )[:hits]


def vmem(count):
    return [pl.BlockSpec(memory_space=pltpu.VMEM)] * count


PARAMS = pltpu.CompilerParams(vmem_limit_bytes=VMEM_BYTES)
ENCODE_PARAMS = pltpu.CompilerParams(vmem_limit_bytes=ENCODE_VMEM_BYTES)


def local(
    pixels,
    stem_weight,
    veto_weight,
    hit_frames,
    assign,
    token_in,
    token_out,
    chan_in,
    chan_out,
    readout,
    latent_gain,
    class_weight,
):
    owners = lax.axis_size("mod")
    streams = lax.axis_size("stream")
    _, frames, height, columns = pixels.shape
    channels = stem_weight.shape[1]
    mix, width = token_in.shape[1:]
    hidden = chan_in.shape[2]
    hits = hit_frames.shape[1]
    hits_owned = hits // owners
    hit_rows = hits_owned * width
    half_rows = hidden + mix * PAD_ROW // LANES
    anywhere = pl.BlockSpec(memory_space=pl.ANY)

    half = jax.ShapeDtypeStruct((half_rows, LANES), BF16)
    mine, other = pl.pallas_call(
        pack_kernel,
        name="pack",
        out_shape=(half, half),
        in_specs=[anywhere] * 4,
        out_specs=vmem(2),
        scratch_shapes=[
            pltpu.VMEM((width, mix), BF16),
            pltpu.VMEM((width, mix), BF16),
            pltpu.SemaphoreType.DMA((3 + hidden // LANES,)),
        ],
        compiler_params=PARAMS,
    )(token_in[0].T, token_out[0], chan_in[0], chan_out[0])
    halves = [mine, other]
    for k in range(1, streams):
        got = lax.ppermute(mine, "stream", [(i, i ^ k) for i in range(streams)])
        halves += [got, lax.ppermute(got, "mod", [(i, i ^ 1) for i in range(owners)])]

    outgoing = pl.pallas_call(
        stem_kernel,
        name="stem",
        out_shape=jax.ShapeDtypeStruct((owners, hit_rows + VETO_ROWS, channels), BF16),
        in_specs=[anywhere] * 4,
        out_specs=vmem(1)[0],
        scratch_shapes=[
            pltpu.VMEM((frames, height, columns), BF16),
            pltpu.VMEM((frames * columns // (2 * PATCH), 2 * PATCH * PATCH), BF16),
            pltpu.VMEM(stem_weight.shape, BF16),
            pltpu.VMEM((2 * PATCH * PATCH, 2 * channels), BF16),
            pltpu.VMEM(veto_weight.shape, F32),
            pltpu.VMEM((1, hits), jnp.int32),
            pltpu.VMEM((hits * width, channels), F32),
            pltpu.SemaphoreType.DMA((4 + 3,)),
        ],
        compiler_params=PARAMS,
        cost_estimate=pl.CostEstimate(flops=5_000_000_000, bytes_accessed=3_000_000, transcendentals=0),
    )(pixels[0], stem_weight, veto_weight, hit_frames)
    received = lax.all_to_all(outgoing, "mod", split_axis=0, concat_axis=0, tiled=True)

    veto, latents, scores = pl.pallas_call(
        functools.partial(encode_kernel, streams, width, hidden),
        name="encode",
        out_shape=(
            jax.ShapeDtypeStruct((1, frames // owners), F32),
            jax.ShapeDtypeStruct((hits_owned, 1, channels), F32),
            jax.ShapeDtypeStruct((hits_owned, 1, class_weight.shape[1]), F32),
        ),
        in_specs=vmem(1)
        + [pl.BlockSpec(memory_space=pltpu.SMEM)]
        + vmem(3)
        + [pl.BlockSpec(memory_space=pl.ANY)] * len(halves),
        out_specs=tuple(vmem(3)),
        scratch_shapes=[
            pltpu.VMEM((streams, 2, half_rows, LANES), BF16),
            pltpu.VMEM((8 * owners, channels), F32),
            pltpu.SemaphoreType.DMA((2 * streams,)),
        ],
        compiler_params=ENCODE_PARAMS,
    )(received, assign.reshape(hits), readout, latent_gain.reshape(1, channels), class_weight.T, *halves)
    return (veto, jnp.swapaxes(latents, 0, 1), jnp.swapaxes(scores, 0, 1))


def solution(mesh):
    in_specs = (
        P("stream", None, "mod", None),
        P(),
        P(),
        P("stream", None),
        P("stream", None, None),
        P("stream", None, None),
        P("stream", None, None),
        P("stream", None, None),
        P("stream", None, None),
        P(),
        P(),
        P(),
    )
    out_specs = (P("stream", "mod"), P("stream", "mod", None), P("stream", "mod", None))
    return jax.shard_map(local, mesh=mesh, in_specs=in_specs, out_specs=out_specs, check_vma=False)
```

```python
import functools
import math

import jax
import jax.numpy as jnp
from jax import lax
from jax.experimental import pallas as pl
from jax.experimental.pallas import tpu as pltpu
from jax.sharding import PartitionSpec as P

PATCH = 16
LANES = 128
GROUP = 16
VETO_ROWS = 16
PAD_ROW = 32
PACK_VMEM_BYTES = 16 * 1024 * 1024
STEM_VMEM_BYTES = 40 * 1024 * 1024
ENCODE_VMEM_BYTES = 32 * 1024 * 1024
F32 = jnp.float32
BF16 = jnp.bfloat16
GELU_A = math.sqrt(2.0 / math.pi)
GELU_B = GELU_A * 0.044715


def gelu(x):
    half = 0.5 * x
    return half + half * jnp.tanh(x * (GELU_A + GELU_B * (x * x)))


def gelu_narrow(x):
    x = x.astype(BF16)
    half = x * BF16(0.5)
    return half + half * jnp.tanh(x * (BF16(GELU_A) + BF16(GELU_B) * (x * x)))


def rms_norm(values):
    return values * lax.rsqrt(jnp.mean(values * values, axis=-1, keepdims=True) + 1e-06)


def dot(a, b):
    return jnp.dot(a, b, preferred_element_type=F32)


def iota(shape, axis):
    return lax.broadcasted_iota(jnp.int32, shape, axis)


def pack_kernel(
    token_in, token_out, chan_in, chan_out, pixels, mine, other, images, token_in_rows, token_out_rows, sems
):
    core = lax.axis_index("mod") % 2
    channels, hidden = chan_in.shape
    width, mix = token_in.shape
    small = (
        pltpu.make_async_copy(token_in, token_in_rows, sems.at[0]),
        pltpu.make_async_copy(token_out, token_out_rows, sems.at[1]),
    )
    for c in small:
        c.start()
    whole = pltpu.make_async_copy(pixels, images, sems.at[3 + hidden // LANES])

    def pack(first, second):
        large = [pltpu.make_async_copy(chan_out, second.at[pl.ds(0, hidden)], sems.at[2])]
        for j in range(hidden // LANES):
            large.append(
                pltpu.make_async_copy(
                    chan_in.at[:, pl.ds(j * LANES, LANES)], first.at[pl.ds(j * channels, channels)], sems.at[3 + j]
                )
            )
        for c in large:
            c.start()
        whole.start()
        for c in small:
            c.wait()
        for source, ref in ((token_in_rows, first), (token_out_rows, second)):
            wide = source[...].astype(F32)
            wide = jnp.concatenate([wide, jnp.zeros((PAD_ROW - width, mix), F32)], axis=0).astype(BF16)
            for j in range(mix // LANES):
                ref[hidden + j * PAD_ROW : hidden + (j + 1) * PAD_ROW, :] = wide[:, j * LANES : (j + 1) * LANES]
        for c in large:
            c.wait()

    @pl.when(core == 0)
    def _():
        pack(mine, other)

    @pl.when(core == 1)
    def _():
        pack(other, mine)

    whole.wait()


def turn(tiles, span):
    count = len(tiles)
    lane = iota(tiles[0].shape, 1)
    size = span * count // 2
    half = count // 2
    while half:
        low = (lane // size) % 2 == 0
        done = list(tiles)
        for i in range(count):
            if i // half % 2 == 0:
                a, b = tiles[i], tiles[i + half]
                done[i] = jnp.where(low, a, roll(b, size))
                done[i + half] = jnp.where(low, roll(a, LANES - size), b)
        tiles, half, size = done, half // 2, size // 2
    return tiles


def roll(x, shift):
    return jnp.concatenate([x[:, LANES - shift :], x[:, : LANES - shift]], axis=1)


def stem_kernel(
    images, weight, veto_weight, hit_frames, out, rows, small, wide, veto_rows, hit_row, chosen, sems
):
    frames, _, columns = images.shape
    owners = out.shape[0]
    hits = hit_frames.shape[1]
    owned = frames // owners
    hit_rows = out.shape[1] - VETO_ROWS
    channels = weight.shape[1]
    blocks = columns // LANES
    quads = LANES // (2 * PATCH)
    tokens = columns // PATCH
    side = [
        pltpu.make_async_copy(weight, small, sems.at[0]),
        pltpu.make_async_copy(veto_weight, veto_rows, sems.at[1]),
        pltpu.make_async_copy(hit_frames, hit_row, sems.at[2]),
    ]
    for c in side:
        c.start()
    size = GROUP * PATCH
    r, c = iota((size, size), 0), iota((size, size), 1)
    swap = (c == (r % GROUP) * PATCH + r // GROUP).astype(F32).astype(BF16)
    batch = math.gcd(frames // GROUP, 6)

    @pl.loop(0, frames // GROUP // batch)
    def _(i):
        for sub in range(batch):
            g = i * batch + sub
            block = images[pl.ds(pl.multiple_of(g * GROUP, GROUP), GROUP)].reshape(size, columns)
            turned = dot(swap, block).astype(BF16)
            for j in range(blocks):
                for p in range(0, PATCH, quads):
                    tiles = [
                        turned[q * GROUP : (q + 1) * GROUP, j * LANES : (j + 1) * LANES] for q in range(p, p + quads)
                    ]
                    for n, tile in enumerate(turn(tiles, 2 * PATCH)):
                        top = pl.multiple_of((n * blocks + j) * frames + g * GROUP, GROUP)
                        rows[pl.ds(top, GROUP), p * 2 * PATCH : p * 2 * PATCH + LANES] = tile

    for c in side:
        c.wait()
    zero = jnp.zeros((PATCH, channels), BF16)
    for p in range(PATCH):
        tile = small[p * PATCH : (p + 1) * PATCH, :]
        for a in range(2):
            top = (p * 2 + a) * PATCH
            for b in range(2):
                wide[top : top + PATCH, b * channels : (b + 1) * channels] = tile if a == b else zero
    pick = (iota((frames, hits), 0) == hit_row[...]).astype(F32).T.astype(BF16)
    sums = jnp.zeros((frames, channels), F32)
    spots = [(n, j) for n in range(quads) for j in range(blocks)]
    parts = [gelu(dot(rows[(n * blocks + j) * frames : (n * blocks + j + 1) * frames, :], wide[...])) for n, j in spots]
    for part in parts:
        sums = sums + part[:, :channels] + part[:, channels:]
    takens = [dot(pick, part.astype(BF16)) for part in parts]
    for (n, j), taken in zip(spots, takens):
        for k in range(2):
            chosen[pl.ds(j * 2 * quads + 2 * n + k, hits, stride=tokens), :] = taken[
                :, k * channels : (k + 1) * channels
            ]
    scale = jnp.broadcast_to(veto_rows[pl.ds(lax.axis_index("mod"), 1), :] / tokens, (VETO_ROWS, channels))
    row = iota((VETO_ROWS, owned), 0)
    for o in range(owners):
        out[o, 0:hit_rows, :] = chosen[o * hit_rows : (o + 1) * hit_rows, :].astype(BF16)
        veto = lax.dot_general(
            scale,
            sums[o * owned : (o + 1) * owned],
            (((1,), (1,)), ((), ())),
            preferred_element_type=F32,
            precision=lax.Precision.HIGHEST,
        )
        high = veto.astype(BF16).astype(F32)
        both = jnp.where(row == 0, high, jnp.where(row == 1, veto - high, 0.0))
        both = jnp.concatenate([both, jnp.zeros((VETO_ROWS, LANES - owned), F32)], axis=1)
        out[o, hit_rows : hit_rows + VETO_ROWS, :] = both.astype(BF16)


def encode_kernel(streams, width, hidden, *refs):
    features, targets, readout, gain, class_weight = refs[:5]
    halves = refs[5 : 5 + 2 * streams]
    veto, latents, scores, table, pools = refs[5 + 2 * streams :]
    owners = features.shape[0]
    channels = features.shape[2]
    hits = latents.shape[0]
    hit_rows = hits * width
    here = lax.axis_index("stream")
    own = lax.axis_index("mod")
    core = own % 2

    @pl.loop(0, hits)
    def _(slot):
        wanted = targets[own * hits + slot] ^ here
        for k in range(streams):

            @pl.when(wanted == k)
            def _():
                table[slot, core] = halves[2 * k][...]
                table[slot, 1 - core] = halves[2 * k + 1][...]

    terms = jnp.sum(features[:, hit_rows : hit_rows + VETO_ROWS, :].astype(F32), axis=0)
    veto[...] = jnp.sum(terms, axis=0, keepdims=True)[:, : veto.shape[1]]
    pools[...] = jnp.zeros_like(pools)

    extra = table.shape[2] - hidden
    blocks = extra // PAD_ROW
    gap = jnp.zeros((PAD_ROW - width, channels), F32)

    def widen(slot, half):
        return jnp.concatenate(
            [table[slot, half, hidden + j * PAD_ROW : hidden + (j + 1) * PAD_ROW, :] for j in range(blocks)], axis=1
        )

    def spread(x):
        normed = rms_norm(x)
        return jnp.concatenate(
            [jnp.concatenate([normed[r], gap], axis=0).astype(BF16) for r in range(owners)], axis=1
        )

    def mix_in(slot, wide):
        token_in = widen(slot, 0).astype(F32).T.astype(BF16)
        return gelu_narrow(dot(token_in, wide))

    def mix_out(slot, x, mixed):
        back = dot(widen(slot, 1), mixed)
        after = jnp.concatenate(
            [x[r] + back[:width, r * channels : (r + 1) * channels] for r in range(owners)], axis=0
        )
        return after.astype(BF16).astype(F32)

    def channel_in(slot, after):
        chan_in = jnp.concatenate(
            [table[slot, 0, j * channels : (j + 1) * channels, :] for j in range(hidden // channels)], axis=1
        )
        return gelu_narrow(dot(rms_norm(after).astype(BF16), chan_in))

    def channel_out(slot, after, inner):
        last = after + dot(inner, table[slot, 1, 0:hidden, :])
        pool = jnp.sum(last.reshape(owners, width, channels), axis=1) * (1.0 / width)
        pools[pl.ds(pl.multiple_of(slot * owners, owners), owners), :] = pool

    group = hits if owners <= 8 else 2

    @pl.loop(0, hits // group)
    def _(i):
        first = i * group
        every = features[:, pl.ds(pl.multiple_of(first * width, 16), group * width), :].astype(F32)
        slots = [first + a for a in range(group)]
        x = [every[:, a * width : (a + 1) * width] for a in range(group)]
        wide = [spread(v) for v in x]
        mixed = [mix_in(n, v) for n, v in zip(slots, wide)]
        after = [mix_out(n, v, m) for n, v, m in zip(slots, x, mixed)]
        inner = [channel_in(n, v) for n, v in zip(slots, after)]
        for n, v, m in zip(slots, after, inner):
            channel_out(n, v, m)

    pooled = jnp.concatenate(
        [pools[pl.ds(r, 8, stride=owners), :].astype(BF16) for r in range(owners)], axis=1
    )
    latent = rms_norm(dot(pooled, readout[...])) * gain[...]
    latents[:, 0, :] = latent[:hits]
    scores[:, 0, :] = lax.dot_general(
        latent,
        class_weight[...],
        (((1,), (1,)), ((), ())),
        preferred_element_type=F32,
        precision=lax.Precision.HIGHEST,
    )[:hits]


def vmem(count):
    return [pl.BlockSpec(memory_space=pltpu.VMEM)] * count


def in_hbm(x):
    return pltpu.with_memory_space_constraint(x, pltpu.HBM)


def local(
    pixels,
    stem_weight,
    veto_weight,
    hit_frames,
    assign,
    token_in,
    token_out,
    chan_in,
    chan_out,
    readout,
    latent_gain,
    class_weight,
):
    owners = lax.axis_size("mod")
    streams = lax.axis_size("stream")
    _, frames, height, columns = pixels.shape
    channels = stem_weight.shape[1]
    mix, width = token_in.shape[1:]
    hidden = chan_in.shape[2]
    hits = hit_frames.shape[1]
    hits_owned = hits // owners
    hit_rows = hits_owned * width
    half_rows = hidden + mix * PAD_ROW // LANES
    anywhere = pl.BlockSpec(memory_space=pl.ANY)

    half = pltpu.VMEM((half_rows, LANES), BF16)
    mine, other, images = pl.pallas_call(
        pack_kernel,
        name="pack",
        out_shape=(half, half, pltpu.VMEM((frames, height, columns), BF16)),
        in_specs=[anywhere] * 5,
        out_specs=vmem(3),
        scratch_shapes=[
            pltpu.VMEM((width, mix), BF16),
            pltpu.VMEM((width, mix), BF16),
            pltpu.SemaphoreType.DMA((4 + hidden // LANES,)),
        ],
        compiler_params=pltpu.CompilerParams(vmem_limit_bytes=PACK_VMEM_BYTES),
    )(in_hbm(token_in[0].T), in_hbm(token_out[0]), in_hbm(chan_in[0]), in_hbm(chan_out[0]), in_hbm(pixels[0]))

    def send(k, rows):
        got = lax.ppermute(rows, "stream", [(i, i ^ k) for i in range(streams)])
        return [got, lax.ppermute(got, "mod", [(i, i ^ 1) for i in range(owners)])]

    halves = {0: [mine, other]} | {k: send(k, mine) for k in range(streams - 1, 0, -1)}
    outgoing = pl.pallas_call(
        stem_kernel,
        name="stem",
        out_shape=jax.ShapeDtypeStruct((owners, hit_rows + VETO_ROWS, channels), BF16),
        in_specs=vmem(1) + [anywhere] * 3,
        out_specs=vmem(1)[0],
        scratch_shapes=[
            pltpu.VMEM((frames * columns // (2 * PATCH), 2 * PATCH * PATCH), BF16),
            pltpu.VMEM(stem_weight.shape, BF16),
            pltpu.VMEM((2 * PATCH * PATCH, 2 * channels), BF16),
            pltpu.VMEM(veto_weight.shape, F32),
            pltpu.VMEM((1, hits), jnp.int32),
            pltpu.VMEM((hits * width, channels), F32),
            pltpu.SemaphoreType.DMA((3,)),
        ],
        compiler_params=pltpu.CompilerParams(vmem_limit_bytes=STEM_VMEM_BYTES),
        cost_estimate=pl.CostEstimate(flops=5_000_000_000, bytes_accessed=3_000_000, transcendentals=0),
    )(images, in_hbm(stem_weight), in_hbm(veto_weight), in_hbm(hit_frames))
    received = lax.all_to_all(outgoing, "mod", split_axis=0, concat_axis=0, tiled=True)
    halves = [ref for k in range(streams) for ref in halves[k]]

    veto, latents, scores = pl.pallas_call(
        functools.partial(encode_kernel, streams, width, hidden),
        name="encode",
        out_shape=(
            jax.ShapeDtypeStruct((1, frames // owners), F32),
            jax.ShapeDtypeStruct((hits_owned, 1, channels), F32),
            jax.ShapeDtypeStruct((hits_owned, 1, class_weight.shape[1]), F32),
        ),
        in_specs=vmem(1)
        + [pl.BlockSpec(memory_space=pltpu.SMEM)]
        + vmem(3 + len(halves)),
        out_specs=tuple(vmem(3)),
        scratch_shapes=[
            pltpu.VMEM((hits_owned, 2, half_rows, LANES), BF16),
            pltpu.VMEM((8 * owners, channels), F32),
        ],
        compiler_params=pltpu.CompilerParams(vmem_limit_bytes=ENCODE_VMEM_BYTES),
    )(received, assign.reshape(hits), readout, latent_gain.reshape(1, channels), class_weight.T, *halves)
    return (veto, jnp.swapaxes(latents, 0, 1), jnp.swapaxes(scores, 0, 1))


def solution(mesh):
    in_specs = (
        P("stream", None, "mod", None),
        P(),
        P(),
        P("stream", None),
        P("stream", None, None),
        P("stream", None, None),
        P("stream", None, None),
        P("stream", None, None),
        P("stream", None, None),
        P(),
        P(),
        P(),
    )
    out_specs = (P("stream", "mod"), P("stream", "mod", None), P("stream", "mod", None))
    return jax.shard_map(local, mesh=mesh, in_specs=in_specs, out_specs=out_specs, check_vma=False)
```

```python
import functools
import math

import jax
import jax.numpy as jnp
from jax import lax
from jax.experimental import pallas as pl
from jax.experimental.pallas import tpu as pltpu
from jax.sharding import PartitionSpec as P

PATCH = 16
LANES = 128
GROUP = 16
VETO_ROWS = 16
PAD_ROW = 32
PACK_VMEM_BYTES = 16 * 1024 * 1024
STEM_VMEM_BYTES = 40 * 1024 * 1024
ENCODE_VMEM_BYTES = 32 * 1024 * 1024
F32 = jnp.float32
BF16 = jnp.bfloat16
GELU_A = math.sqrt(2.0 / math.pi)
GELU_B = GELU_A * 0.044715


def gelu(x):
    half = 0.5 * x
    return half + half * jnp.tanh(x * (GELU_A + GELU_B * (x * x)))


def gelu_narrow(x):
    x = x.astype(BF16)
    half = x * BF16(0.5)
    return half + half * jnp.tanh(x * (BF16(GELU_A) + BF16(GELU_B) * (x * x)))


def rms_norm(values):
    return values * lax.rsqrt(jnp.mean(values * values, axis=-1, keepdims=True) + 1e-06)


def dot(a, b):
    return jnp.dot(a, b, preferred_element_type=F32)


def iota(shape, axis):
    return lax.broadcasted_iota(jnp.int32, shape, axis)


def pack_kernel(
    token_in, token_out, chan_in, chan_out, mine, other, token_in_rows, token_out_rows, sems
):
    core = lax.axis_index("mod") % 2
    channels, hidden = chan_in.shape
    width, mix = token_in.shape
    small = (
        pltpu.make_async_copy(token_in, token_in_rows, sems.at[0]),
        pltpu.make_async_copy(token_out, token_out_rows, sems.at[1]),
    )
    for c in small:
        c.start()

    def pack(first, second):
        large = [pltpu.make_async_copy(chan_out, second.at[pl.ds(0, hidden)], sems.at[2])]
        for j in range(hidden // LANES):
            large.append(
                pltpu.make_async_copy(
                    chan_in.at[:, pl.ds(j * LANES, LANES)], first.at[pl.ds(j * channels, channels)], sems.at[3 + j]
                )
            )
        for c in large:
            c.start()
        for c in small:
            c.wait()
        for source, ref in ((token_in_rows, first), (token_out_rows, second)):
            wide = source[...].astype(F32)
            wide = jnp.concatenate([wide, jnp.zeros((PAD_ROW - width, mix), F32)], axis=0).astype(BF16)
            for j in range(mix // LANES):
                ref[hidden + j * PAD_ROW : hidden + (j + 1) * PAD_ROW, :] = wide[:, j * LANES : (j + 1) * LANES]
        for c in large:
            c.wait()

    @pl.when(core == 0)
    def _():
        pack(mine, other)

    @pl.when(core == 1)
    def _():
        pack(other, mine)


def turn(tiles, span):
    count = len(tiles)
    lane = iota(tiles[0].shape, 1)
    size = span * count // 2
    half = count // 2
    while half:
        low = (lane // size) % 2 == 0
        done = list(tiles)
        for i in range(count):
            if i // half % 2 == 0:
                a, b = tiles[i], tiles[i + half]
                done[i] = jnp.where(low, a, roll(b, size))
                done[i + half] = jnp.where(low, roll(a, LANES - size), b)
        tiles, half, size = done, half // 2, size // 2
    return tiles


def roll(x, shift):
    return jnp.concatenate([x[:, LANES - shift :], x[:, : LANES - shift]], axis=1)


def stem_kernel(
    images, weight, veto_weight, hit_frames, out, rows, small, wide, veto_rows, hit_row, chosen, sems
):
    frames, _, columns = images.shape
    owners = out.shape[0]
    hits = hit_frames.shape[1]
    owned = frames // owners
    hit_rows = out.shape[1] - VETO_ROWS
    channels = weight.shape[1]
    blocks = columns // LANES
    quads = LANES // (2 * PATCH)
    tokens = columns // PATCH
    side = [
        pltpu.make_async_copy(weight, small, sems.at[0]),
        pltpu.make_async_copy(veto_weight, veto_rows, sems.at[1]),
        pltpu.make_async_copy(hit_frames, hit_row, sems.at[2]),
    ]
    for c in side:
        c.start()
    size = GROUP * PATCH
    r, c = iota((size, size), 0), iota((size, size), 1)
    swap = (c == (r % GROUP) * PATCH + r // GROUP).astype(F32).astype(BF16)
    batch = math.gcd(frames // GROUP, 6)

    @pl.loop(0, frames // GROUP // batch)
    def _(i):
        for sub in range(batch):
            g = i * batch + sub
            block = images[pl.ds(pl.multiple_of(g * GROUP, GROUP), GROUP)].reshape(size, columns)
            turned = dot(swap, block).astype(BF16)
            for j in range(blocks):
                for p in range(0, PATCH, quads):
                    tiles = [
                        turned[q * GROUP : (q + 1) * GROUP, j * LANES : (j + 1) * LANES] for q in range(p, p + quads)
                    ]
                    for n, tile in enumerate(turn(tiles, 2 * PATCH)):
                        top = pl.multiple_of((n * blocks + j) * frames + g * GROUP, GROUP)
                        rows[pl.ds(top, GROUP), p * 2 * PATCH : p * 2 * PATCH + LANES] = tile

    for c in side:
        c.wait()
    zero = jnp.zeros((PATCH, channels), BF16)
    for p in range(PATCH):
        tile = small[p * PATCH : (p + 1) * PATCH, :]
        for a in range(2):
            top = (p * 2 + a) * PATCH
            for b in range(2):
                wide[top : top + PATCH, b * channels : (b + 1) * channels] = tile if a == b else zero
    pick = (iota((frames, hits), 0) == hit_row[...]).astype(F32).T.astype(BF16)
    sums = jnp.zeros((frames, channels), F32)
    spots = [(n, j) for n in range(quads) for j in range(blocks)]
    parts = [gelu_narrow(dot(rows[(n * blocks + j) * frames : (n * blocks + j + 1) * frames, :], wide[...])) for n, j in spots]
    for part in parts:
        sums = sums + part[:, :channels].astype(F32) + part[:, channels:].astype(F32)
    takens = [dot(pick, part.astype(BF16)) for part in parts]
    for (n, j), taken in zip(spots, takens):
        for k in range(2):
            chosen[pl.ds(j * 2 * quads + 2 * n + k, hits, stride=tokens), :] = taken[
                :, k * channels : (k + 1) * channels
            ]
    scale = jnp.broadcast_to(veto_rows[pl.ds(lax.axis_index("mod"), 1), :] / tokens, (VETO_ROWS, channels))
    row = iota((VETO_ROWS, owned), 0)
    for o in range(owners):
        out[o, 0:hit_rows, :] = chosen[o * hit_rows : (o + 1) * hit_rows, :].astype(BF16)
        veto = lax.dot_general(
            scale,
            sums[o * owned : (o + 1) * owned],
            (((1,), (1,)), ((), ())),
            preferred_element_type=F32,
            precision=lax.Precision.HIGHEST,
        )
        high = veto.astype(BF16).astype(F32)
        both = jnp.where(row == 0, high, jnp.where(row == 1, veto - high, 0.0))
        both = jnp.concatenate([both, jnp.zeros((VETO_ROWS, LANES - owned), F32)], axis=1)
        out[o, hit_rows : hit_rows + VETO_ROWS, :] = both.astype(BF16)


def encode_kernel(streams, width, hidden, *refs):
    features, targets, readout, gain, class_weight = refs[:5]
    halves = refs[5 : 5 + 2 * streams]
    veto, latents, scores, table, pools = refs[5 + 2 * streams :]
    owners = features.shape[0]
    channels = features.shape[2]
    hits = latents.shape[0]
    hit_rows = hits * width
    here = lax.axis_index("stream")
    own = lax.axis_index("mod")
    core = own % 2

    @pl.loop(0, hits)
    def _(slot):
        wanted = targets[own * hits + slot] ^ here
        for k in range(streams):

            @pl.when(wanted == k)
            def _():
                table[slot, core] = halves[2 * k][...]
                table[slot, 1 - core] = halves[2 * k + 1][...]

    terms = jnp.sum(features[:, hit_rows : hit_rows + VETO_ROWS, :].astype(F32), axis=0)
    veto[...] = jnp.sum(terms, axis=0, keepdims=True)[:, : veto.shape[1]]
    pools[...] = jnp.zeros_like(pools)

    extra = table.shape[2] - hidden
    blocks = extra // PAD_ROW
    gap = jnp.zeros((PAD_ROW - width, channels), F32)

    def widen(slot, half):
        return jnp.concatenate(
            [table[slot, half, hidden + j * PAD_ROW : hidden + (j + 1) * PAD_ROW, :] for j in range(blocks)], axis=1
        )

    def spread(x):
        normed = rms_norm(x)
        return jnp.concatenate(
            [jnp.concatenate([normed[r], gap], axis=0).astype(BF16) for r in range(owners)], axis=1
        )

    def mix_in(slot, wide):
        token_in = widen(slot, 0).astype(F32).T.astype(BF16)
        return gelu_narrow(dot(token_in, wide))

    def mix_out(slot, x, mixed):
        back = dot(widen(slot, 1), mixed)
        after = jnp.concatenate(
            [x[r] + back[:width, r * channels : (r + 1) * channels] for r in range(owners)], axis=0
        )
        return after.astype(BF16).astype(F32)

    def channel_in(slot, after):
        chan_in = jnp.concatenate(
            [table[slot, 0, j * channels : (j + 1) * channels, :] for j in range(hidden // channels)], axis=1
        )
        return gelu_narrow(dot(rms_norm(after).astype(BF16), chan_in))

    def channel_out(slot, after, inner):
        last = after + dot(inner, table[slot, 1, 0:hidden, :])
        pool = jnp.sum(last.reshape(owners, width, channels), axis=1) * (1.0 / width)
        pools[pl.ds(pl.multiple_of(slot * owners, owners), owners), :] = pool

    group = hits if owners <= 8 else 2

    @pl.loop(0, hits // group)
    def _(i):
        first = i * group
        every = features[:, pl.ds(pl.multiple_of(first * width, 16), group * width), :].astype(F32)
        slots = [first + a for a in range(group)]
        x = [every[:, a * width : (a + 1) * width] for a in range(group)]
        wide = [spread(v) for v in x]
        mixed = [mix_in(n, v) for n, v in zip(slots, wide)]
        after = [mix_out(n, v, m) for n, v, m in zip(slots, x, mixed)]
        inner = [channel_in(n, v) for n, v in zip(slots, after)]
        for n, v, m in zip(slots, after, inner):
            channel_out(n, v, m)

    pooled = jnp.concatenate(
        [pools[pl.ds(r, 8, stride=owners), :].astype(BF16) for r in range(owners)], axis=1
    )
    latent = rms_norm(dot(pooled, readout[...])) * gain[...]
    latents[:, 0, :] = latent[:hits]
    scores[:, 0, :] = lax.dot_general(
        latent,
        class_weight[...],
        (((1,), (1,)), ((), ())),
        preferred_element_type=F32,
        precision=lax.Precision.HIGHEST,
    )[:hits]


def vmem(count):
    return [pl.BlockSpec(memory_space=pltpu.VMEM)] * count


def in_vmem(x):
    return pltpu.with_memory_space_constraint(x, pltpu.VMEM)


def in_hbm(x):
    return pltpu.with_memory_space_constraint(x, pltpu.HBM)


def local(
    pixels,
    stem_weight,
    veto_weight,
    hit_frames,
    assign,
    token_in,
    token_out,
    chan_in,
    chan_out,
    readout,
    latent_gain,
    class_weight,
):
    owners = lax.axis_size("mod")
    streams = lax.axis_size("stream")
    _, frames, height, columns = pixels.shape
    channels = stem_weight.shape[1]
    mix, width = token_in.shape[1:]
    hidden = chan_in.shape[2]
    hits = hit_frames.shape[1]
    hits_owned = hits // owners
    hit_rows = hits_owned * width
    half_rows = hidden + mix * PAD_ROW // LANES
    anywhere = pl.BlockSpec(memory_space=pl.ANY)

    half = pltpu.VMEM((half_rows, LANES), BF16)
    mine, other = pl.pallas_call(
        pack_kernel,
        name="pack",
        out_shape=(half, half),
        in_specs=[anywhere] * 4,
        out_specs=vmem(2),
        scratch_shapes=[
            pltpu.VMEM((width, mix), BF16),
            pltpu.VMEM((width, mix), BF16),
            pltpu.SemaphoreType.DMA((4 + hidden // LANES,)),
        ],
        compiler_params=pltpu.CompilerParams(vmem_limit_bytes=PACK_VMEM_BYTES),
        cost_estimate=pl.CostEstimate(flops=5000000000, bytes_accessed=3000000, transcendentals=0),
    )(in_hbm(token_in[0].T), in_hbm(token_out[0]), in_hbm(chan_in[0]), in_hbm(chan_out[0]))

    def send(k, rows):
        got = lax.ppermute(rows, "stream", [(i, i ^ k) for i in range(streams)])
        return [got, lax.ppermute(got, "mod", [(i, i ^ 1) for i in range(owners)])]

    halves = {0: [mine, other]} | {k: send(k, mine) for k in range(streams - 1, 0, -1)}
    outgoing = pl.pallas_call(
        stem_kernel,
        name="stem",
        out_shape=jax.ShapeDtypeStruct((owners, hit_rows + VETO_ROWS, channels), BF16),
        in_specs=vmem(1) + [anywhere] * 3,
        out_specs=vmem(1)[0],
        scratch_shapes=[
            pltpu.VMEM((frames * columns // (2 * PATCH), 2 * PATCH * PATCH), BF16),
            pltpu.VMEM(stem_weight.shape, BF16),
            pltpu.VMEM((2 * PATCH * PATCH, 2 * channels), BF16),
            pltpu.VMEM(veto_weight.shape, F32),
            pltpu.VMEM((1, hits), jnp.int32),
            pltpu.VMEM((hits * width, channels), F32),
            pltpu.SemaphoreType.DMA((3,)),
        ],
        compiler_params=pltpu.CompilerParams(vmem_limit_bytes=STEM_VMEM_BYTES),
        cost_estimate=pl.CostEstimate(flops=5_000_000_000, bytes_accessed=3_000_000, transcendentals=0),
    )(in_vmem(pixels[0]), in_hbm(stem_weight), in_hbm(veto_weight), in_hbm(hit_frames))
    received = lax.all_to_all(outgoing, "mod", split_axis=0, concat_axis=0, tiled=True)
    halves = [ref for k in range(streams) for ref in halves[k]]

    veto, latents, scores = pl.pallas_call(
        functools.partial(encode_kernel, streams, width, hidden),
        name="encode",
        out_shape=(
            jax.ShapeDtypeStruct((1, frames // owners), F32),
            jax.ShapeDtypeStruct((hits_owned, 1, channels), F32),
            jax.ShapeDtypeStruct((hits_owned, 1, class_weight.shape[1]), F32),
        ),
        in_specs=vmem(1)
        + [pl.BlockSpec(memory_space=pltpu.SMEM)]
        + vmem(3 + len(halves)),
        out_specs=tuple(vmem(3)),
        scratch_shapes=[
            pltpu.VMEM((hits_owned, 2, half_rows, LANES), BF16),
            pltpu.VMEM((8 * owners, channels), F32),
        ],
        compiler_params=pltpu.CompilerParams(vmem_limit_bytes=ENCODE_VMEM_BYTES),
    )(received, assign.reshape(hits), readout, latent_gain.reshape(1, channels), class_weight.T, *halves)
    return (veto, jnp.swapaxes(latents, 0, 1), jnp.swapaxes(scores, 0, 1))


def solution(mesh):
    in_specs = (
        P("stream", None, "mod", None),
        P(),
        P(),
        P("stream", None),
        P("stream", None, None),
        P("stream", None, None),
        P("stream", None, None),
        P("stream", None, None),
        P("stream", None, None),
        P(),
        P(),
        P(),
    )
    out_specs = (P("stream", "mod"), P("stream", "mod", None), P("stream", "mod", None))
    return jax.shard_map(local, mesh=mesh, in_specs=in_specs, out_specs=out_specs, check_vma=False)
```

```python
import functools
import math

import jax
import jax.numpy as jnp
from jax import lax
from jax.experimental import pallas as pl
from jax.experimental.pallas import tpu as pltpu
from jax.sharding import PartitionSpec as P

PATCH = 16
LANES = 128
GROUP = 16
VETO_ROWS = 16
PAD_ROW = 32
PACK_VMEM_BYTES = 16 * 1024 * 1024
STEM_VMEM_BYTES = 40 * 1024 * 1024
ENCODE_VMEM_BYTES = 32 * 1024 * 1024
F32 = jnp.float32
BF16 = jnp.bfloat16
GELU_A = math.sqrt(2.0 / math.pi)
GELU_B = GELU_A * 0.044715


def gelu(x):
    half = 0.5 * x
    return half + half * jnp.tanh(x * (GELU_A + GELU_B * (x * x)))


def gelu_narrow(x):
    x = x.astype(BF16)
    half = x * BF16(0.5)
    return half + half * jnp.tanh(x * (BF16(GELU_A) + BF16(GELU_B) * (x * x)))


def rms_norm(values):
    return values * lax.rsqrt(jnp.mean(values * values, axis=-1, keepdims=True) + 1e-06)


def dot(a, b):
    return jnp.dot(a, b, preferred_element_type=F32)


def iota(shape, axis):
    return lax.broadcasted_iota(jnp.int32, shape, axis)


def pack_kernel(
    token_in, token_out, chan_in, chan_out, mine, other, token_in_rows, token_out_rows, sems
):
    core = lax.axis_index("mod") % 2
    channels, hidden = chan_in.shape
    width, mix = token_in.shape
    small = (
        pltpu.make_async_copy(token_in, token_in_rows, sems.at[0]),
        pltpu.make_async_copy(token_out, token_out_rows, sems.at[1]),
    )
    for c in small:
        c.start()

    def pack(first, second):
        large = [pltpu.make_async_copy(chan_out, second.at[pl.ds(0, hidden)], sems.at[2])]
        for j in range(hidden // LANES):
            large.append(
                pltpu.make_async_copy(
                    chan_in.at[:, pl.ds(j * LANES, LANES)], first.at[pl.ds(j * channels, channels)], sems.at[3 + j]
                )
            )
        for c in large:
            c.start()
        for c in small:
            c.wait()
        for source, ref in ((token_in_rows, first), (token_out_rows, second)):
            wide = source[...].astype(F32)
            wide = jnp.concatenate([wide, jnp.zeros((PAD_ROW - width, mix), F32)], axis=0).astype(BF16)
            for j in range(mix // LANES):
                ref[hidden + j * PAD_ROW : hidden + (j + 1) * PAD_ROW, :] = wide[:, j * LANES : (j + 1) * LANES]
        for c in large:
            c.wait()

    @pl.when(core == 0)
    def _():
        pack(mine, other)

    @pl.when(core == 1)
    def _():
        pack(other, mine)


def bundle_kernel(chips, *refs):
    features, out = refs[:chips], refs[-1]
    other = 1 - lax.axis_index("mod") % 2
    size = features[0].shape[1]
    for n, ref in enumerate(features):
        out[n * size : (n + 1) * size, :] = ref[other]


def turn(tiles, span):
    count = len(tiles)
    lane = iota(tiles[0].shape, 1)
    size = span * count // 2
    half = count // 2
    while half:
        low = (lane // size) % 2 == 0
        done = list(tiles)
        for i in range(count):
            if i // half % 2 == 0:
                a, b = tiles[i], tiles[i + half]
                done[i] = jnp.where(low, a, roll(b, size))
                done[i + half] = jnp.where(low, roll(a, LANES - size), b)
        tiles, half, size = done, half // 2, size // 2
    return tiles


def roll(x, shift):
    return jnp.concatenate([x[:, LANES - shift :], x[:, : LANES - shift]], axis=1)


def stem_kernel(
    images, weight, veto_weight, hit_frames, *refs
):
    out, (rows, small, wide, veto_rows, hit_row, chosen, totals, sems) = refs[:-8], refs[-8:]
    frames, _, columns = images.shape
    owners = 2 * len(out)
    hits = hit_frames.shape[1]
    owned = frames // owners
    hit_rows = out[0].shape[1] - VETO_ROWS
    channels = weight.shape[1]
    blocks = columns // LANES
    quads = LANES // (2 * PATCH)
    tokens = columns // PATCH
    side = [
        pltpu.make_async_copy(weight, small, sems.at[0]),
        pltpu.make_async_copy(veto_weight, veto_rows, sems.at[1]),
        pltpu.make_async_copy(hit_frames, hit_row, sems.at[2]),
    ]
    for c in side:
        c.start()
    size = GROUP * PATCH
    r, c = iota((size, size), 0), iota((size, size), 1)
    swap = (c == (r % GROUP) * PATCH + r // GROUP).astype(F32).astype(BF16)
    batch = math.gcd(frames // GROUP, 6)

    @pl.loop(0, frames // GROUP // batch)
    def _(i):
        for sub in range(batch):
            g = i * batch + sub
            block = images[pl.ds(pl.multiple_of(g * GROUP, GROUP), GROUP)].reshape(size, columns)
            turned = dot(swap, block).astype(BF16)
            for j in range(blocks):
                for p in range(0, PATCH, quads):
                    tiles = [
                        turned[q * GROUP : (q + 1) * GROUP, j * LANES : (j + 1) * LANES] for q in range(p, p + quads)
                    ]
                    for n, tile in enumerate(turn(tiles, 2 * PATCH)):
                        top = pl.multiple_of((n * blocks + j) * frames + g * GROUP, GROUP)
                        rows[pl.ds(top, GROUP), p * 2 * PATCH : p * 2 * PATCH + LANES] = tile

    for c in side:
        c.wait()
    zero = jnp.zeros((PATCH, channels), BF16)
    for p in range(PATCH):
        tile = small[p * PATCH : (p + 1) * PATCH, :]
        for a in range(2):
            top = (p * 2 + a) * PATCH
            for b in range(2):
                wide[top : top + PATCH, b * channels : (b + 1) * channels] = tile if a == b else zero
    pick = (iota((frames, hits), 0) == hit_row[...]).astype(F32).T.astype(BF16)
    sums = jnp.zeros((frames, channels), F32)
    spots = [(n, j) for n in range(quads) for j in range(blocks)]
    parts = [gelu_narrow(dot(rows[(n * blocks + j) * frames : (n * blocks + j + 1) * frames, :], wide[...])) for n, j in spots]
    for part in parts:
        sums = sums + part[:, :channels].astype(F32) + part[:, channels:].astype(F32)
    takens = [dot(pick, part.astype(BF16)) for part in parts]
    for (n, j), taken in zip(spots, takens):
        for k in range(2):
            chosen[pl.ds(j * 2 * quads + 2 * n + k, hits, stride=tokens), :] = taken[
                :, k * channels : (k + 1) * channels
            ]
    scale = jnp.broadcast_to(veto_rows[pl.ds(lax.axis_index("mod"), 1), :] / tokens, (VETO_ROWS, channels))
    row = iota((VETO_ROWS, owned), 0)
    totals[...] = sums
    for k in range(owners // 2):
        for core in range(2):
            o = ((lax.axis_index("mod") // 2) ^ k) * 2 + core
            taken = chosen[pl.ds(pl.multiple_of(o * hit_rows, 8), hit_rows), :]
            out[k][core, 0:hit_rows, :] = taken.astype(BF16)
            veto = lax.dot_general(
                scale,
                totals[pl.ds(pl.multiple_of(o * owned, 8), owned), :],
                (((1,), (1,)), ((), ())),
                preferred_element_type=F32,
                precision=lax.Precision.HIGHEST,
            )
            high = veto.astype(BF16).astype(F32)
            both = jnp.where(row == 0, high, jnp.where(row == 1, veto - high, 0.0))
            both = jnp.concatenate([both, jnp.zeros((VETO_ROWS, LANES - owned), F32)], axis=1)
            out[k][core, hit_rows : hit_rows + VETO_ROWS, :] = both.astype(BF16)


def encode_kernel(owners, streams, width, hidden, *refs):
    chips = owners // 2
    received, bundle, refs = refs[:chips], refs[chips], refs[chips + 1 :]
    targets, readout, gain, class_weight = refs[:4]
    halves = refs[4 : 4 + 2 * streams]
    veto, latents, scores, table, pools = refs[4 + 2 * streams :]
    channels = received[0].shape[2]
    hits = latents.shape[0]
    hit_rows = hits * width
    block = hit_rows + VETO_ROWS
    here = lax.axis_index("stream")
    own = lax.axis_index("mod")
    core = own % 2

    @pl.loop(0, hits)
    def _(slot):
        wanted = targets[own * hits + slot] ^ here
        for k in range(streams):

            @pl.when(wanted == k)
            def _():
                table[slot, core] = halves[2 * k][...]
                table[slot, 1 - core] = halves[2 * k + 1][...]

    tails = [ref[core, hit_rows:block, :] for ref in received]
    tails += [bundle[n * block + hit_rows : (n + 1) * block, :] for n in range(chips)]
    terms = sum(tail.astype(F32) for tail in tails)
    veto[...] = jnp.sum(terms, axis=0, keepdims=True)[:, : veto.shape[1]]
    pools[...] = jnp.zeros_like(pools)

    extra = table.shape[2] - hidden
    blocks = extra // PAD_ROW
    gap = jnp.zeros((PAD_ROW - width, channels), F32)

    def widen(slot, half):
        return jnp.concatenate(
            [table[slot, half, hidden + j * PAD_ROW : hidden + (j + 1) * PAD_ROW, :] for j in range(blocks)], axis=1
        )

    def spread(x):
        normed = rms_norm(x)
        return jnp.concatenate(
            [jnp.concatenate([normed[r], gap], axis=0).astype(BF16) for r in range(owners)], axis=1
        )

    def mix_in(slot, wide):
        token_in = widen(slot, 0).astype(F32).T.astype(BF16)
        return gelu_narrow(dot(token_in, wide))

    def mix_out(slot, x, mixed):
        back = dot(widen(slot, 1), mixed)
        after = jnp.concatenate(
            [x[r] + back[:width, r * channels : (r + 1) * channels] for r in range(owners)], axis=0
        )
        return after.astype(BF16).astype(F32)

    def channel_in(slot, after):
        chan_in = jnp.concatenate(
            [table[slot, 0, j * channels : (j + 1) * channels, :] for j in range(hidden // channels)], axis=1
        )
        return gelu_narrow(dot(rms_norm(after).astype(BF16), chan_in))

    def channel_out(slot, after, inner):
        last = after + dot(inner, table[slot, 1, 0:hidden, :])
        pool = jnp.sum(last.reshape(owners, width, channels), axis=1) * (1.0 / width)
        pools[pl.ds(pl.multiple_of(slot * owners, owners), owners), :] = pool

    group = hits if owners <= 8 else 2

    @pl.loop(0, hits // group)
    def _(i):
        first = i * group
        start = pl.multiple_of(first * width, 16)
        every = []
        for n, ref in enumerate(received):
            every.append(ref[core, pl.ds(start, group * width), :].astype(F32))
            every.append(bundle[pl.ds(n * block + start, group * width), :].astype(F32))
        every = jnp.stack(every)
        slots = [first + a for a in range(group)]
        x = [every[:, a * width : (a + 1) * width] for a in range(group)]
        wide = [spread(v) for v in x]
        mixed = [mix_in(n, v) for n, v in zip(slots, wide)]
        after = [mix_out(n, v, m) for n, v, m in zip(slots, x, mixed)]
        inner = [channel_in(n, v) for n, v in zip(slots, after)]
        for n, v, m in zip(slots, after, inner):
            channel_out(n, v, m)

    pooled = jnp.concatenate(
        [pools[pl.ds(r, 8, stride=owners), :].astype(BF16) for r in range(owners)], axis=1
    )
    modules = [((own // 2) ^ (r // 2)) * 2 + (core if r % 2 == 0 else 1 - core) for r in range(owners)]
    weights = [readout[pl.ds(pl.multiple_of(m * channels, channels), channels), :] for m in modules]
    latent = rms_norm(dot(pooled, jnp.concatenate(weights, axis=0))) * gain[...]
    latents[:, 0, :] = latent[:hits]
    scores[:, 0, :] = lax.dot_general(
        latent,
        class_weight[...],
        (((1,), (1,)), ((), ())),
        preferred_element_type=F32,
        precision=lax.Precision.HIGHEST,
    )[:hits]


def vmem(count):
    return [pl.BlockSpec(memory_space=pltpu.VMEM)] * count


def in_vmem(x):
    return pltpu.with_memory_space_constraint(x, pltpu.VMEM)


def in_hbm(x):
    return pltpu.with_memory_space_constraint(x, pltpu.HBM)


def local(
    pixels,
    stem_weight,
    veto_weight,
    hit_frames,
    assign,
    token_in,
    token_out,
    chan_in,
    chan_out,
    readout,
    latent_gain,
    class_weight,
):
    owners = lax.axis_size("mod")
    streams = lax.axis_size("stream")
    _, frames, height, columns = pixels.shape
    channels = stem_weight.shape[1]
    mix, width = token_in.shape[1:]
    hidden = chan_in.shape[2]
    hits = hit_frames.shape[1]
    hits_owned = hits // owners
    hit_rows = hits_owned * width
    half_rows = hidden + mix * PAD_ROW // LANES
    anywhere = pl.BlockSpec(memory_space=pl.ANY)

    half = pltpu.VMEM((half_rows, LANES), BF16)
    mine, other = pl.pallas_call(
        pack_kernel,
        name="pack",
        out_shape=(half, half),
        in_specs=[anywhere] * 4,
        out_specs=vmem(2),
        scratch_shapes=[
            pltpu.VMEM((width, mix), BF16),
            pltpu.VMEM((width, mix), BF16),
            pltpu.SemaphoreType.DMA((4 + hidden // LANES,)),
        ],
        compiler_params=pltpu.CompilerParams(vmem_limit_bytes=PACK_VMEM_BYTES),
        cost_estimate=pl.CostEstimate(flops=5000000000, bytes_accessed=3000000, transcendentals=0),
    )(in_hbm(token_in[0].T), in_hbm(token_out[0]), in_hbm(chan_in[0]), in_hbm(chan_out[0]))

    def cross(x, distance):
        return lax.ppermute(x, "mod", [(i, i ^ distance) for i in range(owners)])

    got = {0: mine}
    for k in sorted(range(1, streams), key=lambda k: k != streams // 2):
        low = k & -k
        pairs = [(i, i ^ low) for i in range(streams)]
        got[k] = lax.ppermute(got[k ^ low], "stream", pairs)
    chips = owners // 2
    outgoing = pl.pallas_call(
        stem_kernel,
        name="stem",
        out_shape=(pltpu.VMEM((2, hit_rows + VETO_ROWS, channels), BF16),) * chips,
        in_specs=vmem(1) + [anywhere] * 3,
        out_specs=vmem(chips),
        scratch_shapes=[
            pltpu.VMEM((frames * columns // (2 * PATCH), 2 * PATCH * PATCH), BF16),
            pltpu.VMEM(stem_weight.shape, BF16),
            pltpu.VMEM((2 * PATCH * PATCH, 2 * channels), BF16),
            pltpu.VMEM(veto_weight.shape, F32),
            pltpu.VMEM((1, hits), jnp.int32),
            pltpu.VMEM((hits * width, channels), F32),
            pltpu.VMEM((frames, channels), F32),
            pltpu.SemaphoreType.DMA((3,)),
        ],
        compiler_params=pltpu.CompilerParams(vmem_limit_bytes=STEM_VMEM_BYTES),
        cost_estimate=pl.CostEstimate(flops=5_000_000_000, bytes_accessed=3_000_000, transcendentals=0),
    )(in_vmem(pixels[0]), in_hbm(stem_weight), in_hbm(veto_weight), in_hbm(hit_frames))
    received = [outgoing[0]] + [cross(outgoing[k], 2 * k) for k in range(1, chips)]
    bundle = pl.pallas_call(
        functools.partial(bundle_kernel, chips),
        name="bundle",
        out_shape=pltpu.VMEM((chips * (hit_rows + VETO_ROWS), LANES), BF16),
        in_specs=vmem(chips + 1),
        out_specs=vmem(1)[0],
        compiler_params=pltpu.CompilerParams(vmem_limit_bytes=PACK_VMEM_BYTES),
        cost_estimate=pl.CostEstimate(flops=1_000_000_000, bytes_accessed=1_000_000, transcendentals=0),
    )(*[in_vmem(x) for x in received], in_vmem(got[1]))
    bundle = cross(bundle, 1)
    halves = [mine, other]
    for k in range(1, streams):
        halves += [got[k], cross(got[k], 1)]

    veto, latents, scores = pl.pallas_call(
        functools.partial(encode_kernel, owners, streams, width, hidden),
        name="encode",
        out_shape=(
            jax.ShapeDtypeStruct((1, frames // owners), F32),
            jax.ShapeDtypeStruct((hits_owned, 1, channels), F32),
            jax.ShapeDtypeStruct((hits_owned, 1, class_weight.shape[1]), F32),
        ),
        in_specs=vmem(chips + 1)
        + [pl.BlockSpec(memory_space=pltpu.SMEM)]
        + vmem(3 + len(halves)),
        out_specs=tuple(vmem(3)),
        scratch_shapes=[
            pltpu.VMEM((hits_owned, 2, half_rows, LANES), BF16),
            pltpu.VMEM((8 * owners, channels), F32),
        ],
        compiler_params=pltpu.CompilerParams(vmem_limit_bytes=ENCODE_VMEM_BYTES),
    )(*received, bundle, assign.reshape(hits), readout, latent_gain.reshape(1, channels), class_weight.T, *halves)
    return (veto, jnp.swapaxes(latents, 0, 1), jnp.swapaxes(scores, 0, 1))


def solution(mesh):
    in_specs = (
        P("stream", None, "mod", None),
        P(),
        P(),
        P("stream", None),
        P("stream", None, None),
        P("stream", None, None),
        P("stream", None, None),
        P("stream", None, None),
        P("stream", None, None),
        P(),
        P(),
        P(),
    )
    out_specs = (P("stream", "mod"), P("stream", "mod", None), P("stream", "mod", None))
    return jax.shard_map(local, mesh=mesh, in_specs=in_specs, out_specs=out_specs, check_vma=False)
```

```python
import functools
import math

import jax
import jax.numpy as jnp
from jax import lax
from jax.experimental import pallas as pl
from jax.experimental.pallas import tpu as pltpu
from jax.sharding import PartitionSpec as P

PATCH = 16
LANES = 128
GROUP = 16
VETO_ROWS = 16
PAD_ROW = 32
PACK_VMEM_BYTES = 16 * 1024 * 1024
STEM_VMEM_BYTES = 40 * 1024 * 1024
ENCODE_VMEM_BYTES = 32 * 1024 * 1024
F32 = jnp.float32
BF16 = jnp.bfloat16
GELU_A = math.sqrt(2.0 / math.pi)
GELU_B = GELU_A * 0.044715


def gelu(x):
    half = 0.5 * x
    return half + half * jnp.tanh(x * (GELU_A + GELU_B * (x * x)))


def double_gelu(x):
    x = x.astype(BF16)
    return x + x * jnp.tanh(x * (BF16(GELU_A) + BF16(GELU_B) * (x * x)))


def rms_norm(values):
    return values * lax.rsqrt(jnp.mean(values * values, axis=-1, keepdims=True) + 1e-06)


def dot(a, b):
    return jnp.dot(a, b, preferred_element_type=F32)


def iota(shape, axis):
    return lax.broadcasted_iota(jnp.int32, shape, axis)


def pack_kernel(
    token_in, token_out, chan_in, chan_out, mine, other, token_in_rows, token_out_rows, sems
):
    core = lax.axis_index("mod") % 2
    channels, hidden = chan_in.shape
    width, mix = token_in.shape
    small = (
        pltpu.make_async_copy(token_in, token_in_rows, sems.at[0]),
        pltpu.make_async_copy(token_out, token_out_rows, sems.at[1]),
    )
    for c in small:
        c.start()

    def pack(first, second):
        large = [pltpu.make_async_copy(chan_out, second.at[pl.ds(0, hidden)], sems.at[2])]
        for j in range(hidden // LANES):
            large.append(
                pltpu.make_async_copy(
                    chan_in.at[:, pl.ds(j * LANES, LANES)], first.at[pl.ds(j * channels, channels)], sems.at[3 + j]
                )
            )
        for c in large:
            c.start()
        for c in small:
            c.wait()
        for source, ref in ((token_in_rows, first), (token_out_rows, second)):
            wide = source[...].astype(F32)
            wide = jnp.concatenate([wide, jnp.zeros((PAD_ROW - width, mix), F32)], axis=0).astype(BF16)
            for j in range(mix // LANES):
                ref[hidden + j * PAD_ROW : hidden + (j + 1) * PAD_ROW, :] = wide[:, j * LANES : (j + 1) * LANES]
        for c in large:
            c.wait()

    @pl.when(core == 0)
    def _():
        pack(mine, other)

    @pl.when(core == 1)
    def _():
        pack(other, mine)


def bundle_kernel(chips, *refs):
    features, out = refs[:chips], refs[-1]
    other = 1 - lax.axis_index("mod") % 2
    size = features[0].shape[1]
    for place, ref in enumerate(features):
        n = chips - 1 - place
        out[n * size : (n + 1) * size, :] = ref[other]


def turn(tiles, span):
    count = len(tiles)
    lane = iota(tiles[0].shape, 1)
    size = span * count // 2
    half = count // 2
    while half:
        low = (lane // size) % 2 == 0
        done = list(tiles)
        for i in range(count):
            if i // half % 2 == 0:
                a, b = tiles[i], tiles[i + half]
                done[i] = jnp.where(low, a, roll(b, size))
                done[i + half] = jnp.where(low, roll(a, LANES - size), b)
        tiles, half, size = done, half // 2, size // 2
    return tiles


def roll(x, shift):
    return jnp.concatenate([x[:, LANES - shift :], x[:, : LANES - shift]], axis=1)


def stem_kernel(
    images, weight, veto_weight, hit_frames, *refs
):
    out, (rows, small, wide, veto_rows, hit_row, chosen, totals, sems) = refs[:-8], refs[-8:]
    frames, _, columns = images.shape
    owners = 2 * len(out)
    hits = hit_frames.shape[1]
    owned = frames // owners
    hit_rows = out[0].shape[1] - VETO_ROWS
    channels = weight.shape[1]
    blocks = columns // LANES
    quads = LANES // (2 * PATCH)
    tokens = columns // PATCH
    side = [
        pltpu.make_async_copy(weight, small, sems.at[0]),
        pltpu.make_async_copy(veto_weight, veto_rows, sems.at[1]),
        pltpu.make_async_copy(hit_frames, hit_row, sems.at[2]),
    ]
    for c in side:
        c.start()
    size = GROUP * PATCH
    r, c = iota((size, size), 0), iota((size, size), 1)
    swap = (c == (r % GROUP) * PATCH + r // GROUP).astype(F32).astype(BF16)
    batch = math.gcd(frames // GROUP, 6)

    @pl.loop(0, frames // GROUP // batch)
    def _(i):
        for sub in range(batch):
            g = i * batch + sub
            block = images[pl.ds(pl.multiple_of(g * GROUP, GROUP), GROUP)].reshape(size, columns)
            turned = dot(swap, block).astype(BF16)
            for j in range(blocks):
                for p in range(0, PATCH, quads):
                    tiles = [
                        turned[q * GROUP : (q + 1) * GROUP, j * LANES : (j + 1) * LANES] for q in range(p, p + quads)
                    ]
                    for n, tile in enumerate(turn(tiles, 2 * PATCH)):
                        top = pl.multiple_of((n * blocks + j) * frames + g * GROUP, GROUP)
                        rows[pl.ds(top, GROUP), p * 2 * PATCH : p * 2 * PATCH + LANES] = tile

    for c in side:
        c.wait()
    zero = jnp.zeros((PATCH, channels), BF16)
    for p in range(PATCH):
        tile = small[p * PATCH : (p + 1) * PATCH, :]
        for a in range(2):
            top = (p * 2 + a) * PATCH
            for b in range(2):
                wide[top : top + PATCH, b * channels : (b + 1) * channels] = tile if a == b else zero
    pick = (iota((frames, hits), 0) == hit_row[...]).astype(F32).T.astype(BF16)
    sums = jnp.zeros((frames, channels), F32)
    spots = [(n, j) for n in range(quads) for j in range(blocks)]
    parts = [double_gelu(dot(rows[(n * blocks + j) * frames : (n * blocks + j + 1) * frames, :], wide[...])) for n, j in spots]
    for part in parts:
        sums = sums + part[:, :channels].astype(F32) + part[:, channels:].astype(F32)
    takens = [dot(pick, part.astype(BF16)) for part in parts]
    for (n, j), taken in zip(spots, takens):
        for k in range(2):
            chosen[pl.ds(j * 2 * quads + 2 * n + k, hits, stride=tokens), :] = taken[
                :, k * channels : (k + 1) * channels
            ]
    scale = jnp.broadcast_to(veto_rows[pl.ds(lax.axis_index("mod"), 1), :] / (2 * tokens), (VETO_ROWS, channels))
    row = iota((VETO_ROWS, owned), 0)
    totals[...] = sums
    for k in range(owners // 2):
        for core in range(2):
            o = ((lax.axis_index("mod") // 2) ^ k) * 2 + core
            taken = 0.5 * chosen[pl.ds(pl.multiple_of(o * hit_rows, 8), hit_rows), :]
            out[k][core, 0:hit_rows, :] = taken.astype(BF16)
            veto = lax.dot_general(
                scale,
                totals[pl.ds(pl.multiple_of(o * owned, 8), owned), :],
                (((1,), (1,)), ((), ())),
                preferred_element_type=F32,
                precision=lax.Precision.HIGHEST,
            )
            high = veto.astype(BF16).astype(F32)
            both = jnp.where(row == 0, high, jnp.where(row == 1, veto - high, 0.0))
            both = jnp.concatenate([both, jnp.zeros((VETO_ROWS, LANES - owned), F32)], axis=1)
            out[k][core, hit_rows : hit_rows + VETO_ROWS, :] = both.astype(BF16)


def encode_kernel(owners, streams, width, hidden, *refs):
    chips = owners // 2
    received, bundle, refs = refs[:chips][::-1], refs[chips], refs[chips + 1 :]
    targets, readout, gain, class_weight = refs[:4]
    halves = refs[4 : 4 + 2 * streams]
    veto, latents, scores, table, pools = refs[4 + 2 * streams :]
    channels = received[0].shape[2]
    hits = latents.shape[0]
    hit_rows = hits * width
    block = hit_rows + VETO_ROWS
    here = lax.axis_index("stream")
    own = lax.axis_index("mod")
    core = own % 2

    @pl.loop(0, hits)
    def _(slot):
        wanted = targets[own * hits + slot] ^ here
        for k in range(streams):

            @pl.when(wanted == k)
            def _():
                table[slot, core] = halves[2 * k][...]
                table[slot, 1 - core] = halves[2 * k + 1][...]

    tails = [ref[core, hit_rows:block, :] for ref in received]
    tails += [bundle[n * block + hit_rows : (n + 1) * block, :] for n in range(chips)]
    terms = sum(tail.astype(F32) for tail in tails)
    veto[...] = jnp.sum(terms, axis=0, keepdims=True)[:, : veto.shape[1]]
    pools[...] = jnp.zeros_like(pools)

    extra = table.shape[2] - hidden
    blocks = extra // PAD_ROW
    gap = jnp.zeros((PAD_ROW - width, channels), F32)

    def widen(slot, half):
        return jnp.concatenate(
            [table[slot, half, hidden + j * PAD_ROW : hidden + (j + 1) * PAD_ROW, :] for j in range(blocks)], axis=1
        )

    def spread(x):
        normed = rms_norm(x)
        return jnp.concatenate(
            [jnp.concatenate([normed[r], gap], axis=0).astype(BF16) for r in range(owners)], axis=1
        )

    def mix_in(slot, wide):
        token_in = widen(slot, 0).astype(F32).T.astype(BF16)
        return double_gelu(dot(token_in, wide))

    def mix_out(slot, x, mixed):
        back = 0.5 * dot(widen(slot, 1), mixed)
        after = jnp.concatenate(
            [x[r] + back[:width, r * channels : (r + 1) * channels] for r in range(owners)], axis=0
        )
        return after.astype(BF16).astype(F32)

    def channel_in(slot, after):
        chan_in = jnp.concatenate(
            [table[slot, 0, j * channels : (j + 1) * channels, :] for j in range(hidden // channels)], axis=1
        )
        return double_gelu(dot(rms_norm(after).astype(BF16), chan_in))

    def channel_out(slot, after, inner):
        last = after + 0.5 * dot(inner, table[slot, 1, 0:hidden, :])
        pool = jnp.sum(last.reshape(owners, width, channels), axis=1) * (1.0 / width)
        pools[pl.ds(pl.multiple_of(slot * owners, owners), owners), :] = pool

    group = hits if owners <= 8 else 2

    @pl.loop(0, hits // group)
    def _(i):
        first = i * group
        start = pl.multiple_of(first * width, 16)
        every = []
        for n, ref in enumerate(received):
            every.append(ref[core, pl.ds(start, group * width), :].astype(F32))
            every.append(bundle[pl.ds(n * block + start, group * width), :].astype(F32))
        every = jnp.stack(every)
        slots = [first + a for a in range(group)]
        x = [every[:, a * width : (a + 1) * width] for a in range(group)]
        wide = [spread(v) for v in x]
        mixed = [mix_in(n, v) for n, v in zip(slots, wide)]
        after = [mix_out(n, v, m) for n, v, m in zip(slots, x, mixed)]
        inner = [channel_in(n, v) for n, v in zip(slots, after)]
        for n, v, m in zip(slots, after, inner):
            channel_out(n, v, m)

    pooled = jnp.concatenate(
        [pools[pl.ds(r, 8, stride=owners), :].astype(BF16) for r in range(owners)], axis=1
    )
    modules = [((own // 2) ^ (r // 2)) * 2 + (core if r % 2 == 0 else 1 - core) for r in range(owners)]
    weights = [readout[pl.ds(pl.multiple_of(m * channels, channels), channels), :] for m in modules]
    latent = rms_norm(dot(pooled, jnp.concatenate(weights, axis=0))) * gain[...]
    latents[:, 0, :] = latent[:hits]
    scores[:, 0, :] = lax.dot_general(
        latent,
        class_weight[...],
        (((1,), (1,)), ((), ())),
        preferred_element_type=F32,
        precision=lax.Precision.HIGHEST,
    )[:hits]


def vmem(count):
    return [pl.BlockSpec(memory_space=pltpu.VMEM)] * count


def in_vmem(x):
    return pltpu.with_memory_space_constraint(x, pltpu.VMEM)


def in_hbm(x):
    return pltpu.with_memory_space_constraint(x, pltpu.HBM)


def local(
    pixels,
    stem_weight,
    veto_weight,
    hit_frames,
    assign,
    token_in,
    token_out,
    chan_in,
    chan_out,
    readout,
    latent_gain,
    class_weight,
):
    owners = lax.axis_size("mod")
    streams = lax.axis_size("stream")
    _, frames, height, columns = pixels.shape
    channels = stem_weight.shape[1]
    mix, width = token_in.shape[1:]
    hidden = chan_in.shape[2]
    hits = hit_frames.shape[1]
    hits_owned = hits // owners
    hit_rows = hits_owned * width
    half_rows = hidden + mix * PAD_ROW // LANES
    anywhere = pl.BlockSpec(memory_space=pl.ANY)

    half = pltpu.VMEM((half_rows, LANES), BF16)
    mine, other = pl.pallas_call(
        pack_kernel,
        name="pack",
        out_shape=(half, half),
        in_specs=[anywhere] * 4,
        out_specs=vmem(2),
        scratch_shapes=[
            pltpu.VMEM((width, mix), BF16),
            pltpu.VMEM((width, mix), BF16),
            pltpu.SemaphoreType.DMA((4 + hidden // LANES,)),
        ],
        compiler_params=pltpu.CompilerParams(vmem_limit_bytes=PACK_VMEM_BYTES),
        cost_estimate=pl.CostEstimate(flops=5000000000, bytes_accessed=3000000, transcendentals=0),
    )(in_hbm(token_in[0].T), in_hbm(token_out[0]), in_hbm(chan_in[0]), in_hbm(chan_out[0]))

    def cross(x, distance):
        return lax.ppermute(x, "mod", [(i, i ^ distance) for i in range(owners)])

    got = {0: mine}
    for k in sorted(range(1, streams), key=lambda k: k != streams // 2):
        low = k & -k
        pairs = [(i, i ^ low) for i in range(streams)]
        got[k] = lax.ppermute(got[k ^ low], "stream", pairs)
    chips = owners // 2
    outgoing = pl.pallas_call(
        stem_kernel,
        name="stem",
        out_shape=(pltpu.VMEM((2, hit_rows + VETO_ROWS, channels), BF16),) * chips,
        in_specs=vmem(1) + [anywhere] * 3,
        out_specs=vmem(chips),
        scratch_shapes=[
            pltpu.VMEM((frames * columns // (2 * PATCH), 2 * PATCH * PATCH), BF16),
            pltpu.VMEM(stem_weight.shape, BF16),
            pltpu.VMEM((2 * PATCH * PATCH, 2 * channels), BF16),
            pltpu.VMEM(veto_weight.shape, F32),
            pltpu.VMEM((1, hits), jnp.int32),
            pltpu.VMEM((hits * width, channels), F32),
            pltpu.VMEM((frames, channels), F32),
            pltpu.SemaphoreType.DMA((3,)),
        ],
        compiler_params=pltpu.CompilerParams(vmem_limit_bytes=STEM_VMEM_BYTES),
        cost_estimate=pl.CostEstimate(flops=5_000_000_000, bytes_accessed=3_000_000, transcendentals=0),
    )(in_vmem(pixels[0]), in_hbm(stem_weight), in_hbm(veto_weight), in_hbm(hit_frames))
    received = [outgoing[0]] + [cross(outgoing[k], 2 * k) for k in range(1, chips)]
    bundle = pl.pallas_call(
        functools.partial(bundle_kernel, chips),
        name="bundle",
        out_shape=pltpu.VMEM((chips * (hit_rows + VETO_ROWS), LANES), BF16),
        in_specs=vmem(chips + 1),
        out_specs=vmem(1)[0],
        compiler_params=pltpu.CompilerParams(vmem_limit_bytes=PACK_VMEM_BYTES),
        cost_estimate=pl.CostEstimate(flops=1_000_000_000, bytes_accessed=1_000_000, transcendentals=0),
    )(*[in_vmem(x) for x in received[::-1]], in_vmem(got[1]))
    bundle = cross(bundle, 1)
    halves = [mine, other]
    for k in range(1, streams):
        halves += [got[k], cross(got[k], 1)]

    veto, latents, scores = pl.pallas_call(
        functools.partial(encode_kernel, owners, streams, width, hidden),
        name="encode",
        out_shape=(
            jax.ShapeDtypeStruct((1, frames // owners), F32),
            jax.ShapeDtypeStruct((hits_owned, 1, channels), F32),
            jax.ShapeDtypeStruct((hits_owned, 1, class_weight.shape[1]), F32),
        ),
        in_specs=vmem(chips + 1)
        + [pl.BlockSpec(memory_space=pltpu.SMEM)]
        + vmem(3 + len(halves)),
        out_specs=tuple(vmem(3)),
        scratch_shapes=[
            pltpu.VMEM((hits_owned, 2, half_rows, LANES), BF16),
            pltpu.VMEM((8 * owners, channels), F32),
        ],
        compiler_params=pltpu.CompilerParams(vmem_limit_bytes=ENCODE_VMEM_BYTES),
    )(*received[::-1], bundle, assign.reshape(hits), readout, latent_gain.reshape(1, channels), class_weight.T, *halves)
    return (veto, jnp.swapaxes(latents, 0, 1), jnp.swapaxes(scores, 0, 1))


def solution(mesh):
    in_specs = (
        P("stream", None, "mod", None),
        P(),
        P(),
        P("stream", None),
        P("stream", None, None),
        P("stream", None, None),
        P("stream", None, None),
        P("stream", None, None),
        P("stream", None, None),
        P(),
        P(),
        P(),
    )
    out_specs = (P("stream", "mod"), P("stream", "mod", None), P("stream", "mod", None))
    return jax.shard_map(local, mesh=mesh, in_specs=in_specs, out_specs=out_specs, check_vma=False)
```

```python
import functools
import math

import jax
import jax.numpy as jnp
from jax import lax
from jax.experimental import pallas as pl
from jax.experimental.pallas import tpu as pltpu
from jax.sharding import PartitionSpec as P

PATCH = 16
LANES = 128
GROUP = 16
VETO_ROWS = 16
PAD_ROW = 32
PACK_VMEM_BYTES = 16 * 1024 * 1024
STEM_VMEM_BYTES = 40 * 1024 * 1024
ENCODE_VMEM_BYTES = 32 * 1024 * 1024
F32 = jnp.float32
BF16 = jnp.bfloat16
GELU_A = math.sqrt(2.0 / math.pi)
GELU_B = GELU_A * 0.044715


def gelu(x):
    half = 0.5 * x
    return half + half * jnp.tanh(x * (GELU_A + GELU_B * (x * x)))


def double_gelu(x):
    x = x.astype(BF16)
    return x + x * jnp.tanh(x * (BF16(GELU_A) + BF16(GELU_B) * (x * x)))


def rms_norm(values):
    return values * lax.rsqrt(jnp.mean(values * values, axis=-1, keepdims=True) + 1e-06)


def dot(a, b):
    return jnp.dot(a, b, preferred_element_type=F32)


def iota(shape, axis):
    return lax.broadcasted_iota(jnp.int32, shape, axis)


def pack_kernel(
    token_in, token_out, chan_in, chan_out, mine, other, token_in_rows, token_out_rows, sems
):
    core = lax.axis_index("mod") % 2
    channels, hidden = chan_in.shape
    width, mix = token_in.shape
    small = (
        pltpu.make_async_copy(token_in, token_in_rows, sems.at[0]),
        pltpu.make_async_copy(token_out, token_out_rows, sems.at[1]),
    )
    for c in small:
        c.start()

    def pack(first, second):
        large = [pltpu.make_async_copy(chan_out, second.at[pl.ds(0, hidden)], sems.at[2])]
        for j in range(hidden // LANES):
            large.append(
                pltpu.make_async_copy(
                    chan_in.at[:, pl.ds(j * LANES, LANES)], first.at[pl.ds(j * channels, channels)], sems.at[3 + j]
                )
            )
        for c in large:
            c.start()
        for c in small:
            c.wait()
        for source, ref in ((token_in_rows, first), (token_out_rows, second)):
            wide = source[...].astype(F32)
            wide = jnp.concatenate([wide, jnp.zeros((PAD_ROW - width, mix), F32)], axis=0).astype(BF16)
            for j in range(mix // LANES):
                ref[hidden + j * PAD_ROW : hidden + (j + 1) * PAD_ROW, :] = wide[:, j * LANES : (j + 1) * LANES]
        for c in large:
            c.wait()

    @pl.when(core == 0)
    def _():
        pack(mine, other)

    @pl.when(core == 1)
    def _():
        pack(other, mine)


def bundle_kernel(chips, *refs):
    features, out = refs[:chips], refs[-1]
    other = 1 - lax.axis_index("mod") % 2
    size = features[0].shape[1]
    for place, ref in enumerate(features):
        n = chips - 1 - place
        out[n * size : (n + 1) * size, :] = ref[other]


def turn(tiles, span):
    count = len(tiles)
    lane = iota(tiles[0].shape, 1)
    size = span * count // 2
    half = count // 2
    while half:
        low = (lane // size) % 2 == 0
        done = list(tiles)
        for i in range(count):
            if i // half % 2 == 0:
                a, b = tiles[i], tiles[i + half]
                done[i] = jnp.where(low, a, roll(b, size))
                done[i + half] = jnp.where(low, roll(a, LANES - size), b)
        tiles, half, size = done, half // 2, size // 2
    return tiles


def roll(x, shift):
    return jnp.concatenate([x[:, LANES - shift :], x[:, : LANES - shift]], axis=1)


def stem_kernel(
    images, weight, veto_weight, hit_frames, *refs
):
    out, (rows, small, wide, veto_rows, hit_row, chosen, totals, sems) = refs[:-8], refs[-8:]
    frames, _, columns = images.shape
    owners = 2 * len(out)
    hits = hit_frames.shape[1]
    owned = frames // owners
    hit_rows = out[0].shape[1] - VETO_ROWS
    channels = weight.shape[1]
    blocks = columns // LANES
    quads = LANES // (2 * PATCH)
    tokens = columns // PATCH
    side = [
        pltpu.make_async_copy(weight, small, sems.at[0]),
        pltpu.make_async_copy(veto_weight, veto_rows, sems.at[1]),
        pltpu.make_async_copy(hit_frames, hit_row, sems.at[2]),
    ]
    for c in side:
        c.start()
    size = GROUP * PATCH
    r, c = iota((size, size), 0), iota((size, size), 1)
    swap = (c == (r % GROUP) * PATCH + r // GROUP).astype(F32).astype(BF16)
    batch = math.gcd(frames // GROUP, 6)

    @pl.loop(0, frames // GROUP // batch)
    def _(i):
        for sub in range(batch):
            g = i * batch + sub
            block = images[pl.ds(pl.multiple_of(g * GROUP, GROUP), GROUP)].reshape(size, columns)
            turned = dot(swap, block).astype(BF16)
            for j in range(blocks):
                for p in range(0, PATCH, quads):
                    tiles = [
                        turned[q * GROUP : (q + 1) * GROUP, j * LANES : (j + 1) * LANES] for q in range(p, p + quads)
                    ]
                    for n, tile in enumerate(turn(tiles, 2 * PATCH)):
                        top = pl.multiple_of((n * blocks + j) * frames + g * GROUP, GROUP)
                        rows[pl.ds(top, GROUP), p * 2 * PATCH : p * 2 * PATCH + LANES] = tile

    for c in side:
        c.wait()
    zero = jnp.zeros((PATCH, channels), BF16)
    for p in range(PATCH):
        tile = small[p * PATCH : (p + 1) * PATCH, :]
        for a in range(2):
            top = (p * 2 + a) * PATCH
            for b in range(2):
                wide[top : top + PATCH, b * channels : (b + 1) * channels] = tile if a == b else zero
    pick = (iota((frames, hits), 0) == hit_row[...]).astype(F32).T.astype(BF16)
    sums = jnp.zeros((frames, channels), F32)
    spots = [(n, j) for n in range(quads) for j in range(blocks)]
    parts = [double_gelu(dot(rows[(n * blocks + j) * frames : (n * blocks + j + 1) * frames, :], wide[...])) for n, j in spots]
    for part in parts:
        sums = sums + part[:, :channels].astype(F32) + part[:, channels:].astype(F32)
    takens = [dot(pick, part.astype(BF16)) for part in parts]
    for (n, j), taken in zip(spots, takens):
        for k in range(2):
            chosen[pl.ds(j * 2 * quads + 2 * n + k, hits, stride=tokens), :] = taken[
                :, k * channels : (k + 1) * channels
            ]
    scale = jnp.broadcast_to(veto_rows[pl.ds(lax.axis_index("mod"), 1), :] / (2 * tokens), (VETO_ROWS, channels))
    row = iota((VETO_ROWS, owned), 0)
    totals[...] = sums
    for k in range(owners // 2):
        for core in range(2):
            o = ((lax.axis_index("mod") // 2) ^ k) * 2 + core
            taken = 0.5 * chosen[pl.ds(pl.multiple_of(o * hit_rows, 8), hit_rows), :]
            out[k][core, 0:hit_rows, :] = taken.astype(BF16)
            veto = lax.dot_general(
                scale,
                totals[pl.ds(pl.multiple_of(o * owned, 8), owned), :],
                (((1,), (1,)), ((), ())),
                preferred_element_type=F32,
                precision=lax.Precision.HIGHEST,
            )
            high = veto.astype(BF16).astype(F32)
            both = jnp.where(row == 0, high, jnp.where(row == 1, veto - high, 0.0))
            both = jnp.concatenate([both, jnp.zeros((VETO_ROWS, LANES - owned), F32)], axis=1)
            out[k][core, hit_rows : hit_rows + VETO_ROWS, :] = both.astype(BF16)


def prepare_kernel(width, *refs):
    chips = len(refs) - 3
    received, bundle, wides, veto = refs[:chips][::-1], refs[chips], refs[chips + 1], refs[chips + 2]
    core = lax.axis_index("mod") % 2
    hits = wides.shape[0]
    channels = received[0].shape[2]
    hit_rows = hits * width
    block = hit_rows + VETO_ROWS
    gap = jnp.zeros((hits, PAD_ROW - width, channels), F32)
    for n, ref in enumerate(received):
        parts = (ref[core, 0:hit_rows, :], bundle[n * block : n * block + hit_rows, :])
        for c, part in enumerate(parts):
            normed = rms_norm(part.astype(F32).reshape(hits, width, channels))
            r = 2 * n + c
            wides[:, :, r * channels : (r + 1) * channels] = jnp.concatenate([normed, gap], axis=1).astype(BF16)
    tails = [ref[core, hit_rows:block, :] for ref in received]
    tails += [bundle[n * block + hit_rows : (n + 1) * block, :] for n in range(chips)]
    terms = sum(tail.astype(F32) for tail in tails)
    veto[...] = jnp.sum(terms, axis=0, keepdims=True)[:, : veto.shape[1]]


def encode_kernel(owners, streams, width, hidden, *refs):
    chips = owners // 2
    received, bundle, wides, refs = refs[:chips][::-1], refs[chips], refs[chips + 1], refs[chips + 2 :]
    targets, readout, gain, class_weight = refs[:4]
    halves = refs[4 : 4 + 2 * streams]
    latents, scores, table, pools = refs[4 + 2 * streams :]
    channels = received[0].shape[2]
    hits = latents.shape[0]
    hit_rows = hits * width
    block = hit_rows + VETO_ROWS
    here = lax.axis_index("stream")
    own = lax.axis_index("mod")
    core = own % 2

    @pl.loop(0, hits)
    def _(slot):
        wanted = targets[own * hits + slot] ^ here
        for k in range(streams):

            @pl.when(wanted == k)
            def _():
                table[slot, core] = halves[2 * k][...]
                table[slot, 1 - core] = halves[2 * k + 1][...]

    pools[...] = jnp.zeros_like(pools)

    extra = table.shape[2] - hidden
    blocks = extra // PAD_ROW

    def widen(slot, half):
        return jnp.concatenate(
            [table[slot, half, hidden + j * PAD_ROW : hidden + (j + 1) * PAD_ROW, :] for j in range(blocks)], axis=1
        )

    def mix_in(slot):
        token_in = widen(slot, 0).astype(F32).T.astype(BF16)
        return double_gelu(dot(token_in, wides[slot]))

    def mix_out(slot, x, mixed):
        back = 0.5 * dot(widen(slot, 1), mixed)
        after = jnp.concatenate(
            [x[r] + back[:width, r * channels : (r + 1) * channels] for r in range(owners)], axis=0
        )
        return after.astype(BF16).astype(F32)

    def channel_in(slot, after):
        chan_in = jnp.concatenate(
            [table[slot, 0, j * channels : (j + 1) * channels, :] for j in range(hidden // channels)], axis=1
        )
        return double_gelu(dot(rms_norm(after).astype(BF16), chan_in))

    def channel_out(slot, after, inner):
        last = after + 0.5 * dot(inner, table[slot, 1, 0:hidden, :])
        pool = jnp.sum(last.reshape(owners, width, channels), axis=1) * (1.0 / width)
        pools[pl.ds(pl.multiple_of(slot * owners, owners), owners), :] = pool

    group = hits if owners <= 8 else 2

    @pl.loop(0, hits // group)
    def _(i):
        first = i * group
        start = pl.multiple_of(first * width, 16)
        every = []
        for n, ref in enumerate(received):
            every.append(ref[core, pl.ds(start, group * width), :].astype(F32))
            every.append(bundle[pl.ds(n * block + start, group * width), :].astype(F32))
        every = jnp.stack(every)
        slots = [first + a for a in range(group)]
        x = [every[:, a * width : (a + 1) * width] for a in range(group)]
        mixed = [mix_in(n) for n in slots]
        after = [mix_out(n, v, m) for n, v, m in zip(slots, x, mixed)]
        inner = [channel_in(n, v) for n, v in zip(slots, after)]
        for n, v, m in zip(slots, after, inner):
            channel_out(n, v, m)

    pooled = jnp.concatenate(
        [pools[pl.ds(r, 8, stride=owners), :].astype(BF16) for r in range(owners)], axis=1
    )
    modules = [((own // 2) ^ (r // 2)) * 2 + (core if r % 2 == 0 else 1 - core) for r in range(owners)]
    weights = [readout[pl.ds(pl.multiple_of(m * channels, channels), channels), :] for m in modules]
    latent = rms_norm(dot(pooled, jnp.concatenate(weights, axis=0))) * gain[...]
    latents[:, 0, :] = latent[:hits]
    scores[:, 0, :] = lax.dot_general(
        latent,
        class_weight[...],
        (((1,), (1,)), ((), ())),
        preferred_element_type=F32,
        precision=lax.Precision.HIGHEST,
    )[:hits]


def vmem(count):
    return [pl.BlockSpec(memory_space=pltpu.VMEM)] * count


def in_vmem(x):
    return pltpu.with_memory_space_constraint(x, pltpu.VMEM)


def in_hbm(x):
    return pltpu.with_memory_space_constraint(x, pltpu.HBM)


def local(
    pixels,
    stem_weight,
    veto_weight,
    hit_frames,
    assign,
    token_in,
    token_out,
    chan_in,
    chan_out,
    readout,
    latent_gain,
    class_weight,
):
    owners = lax.axis_size("mod")
    streams = lax.axis_size("stream")
    _, frames, height, columns = pixels.shape
    channels = stem_weight.shape[1]
    mix, width = token_in.shape[1:]
    hidden = chan_in.shape[2]
    hits = hit_frames.shape[1]
    hits_owned = hits // owners
    hit_rows = hits_owned * width
    half_rows = hidden + mix * PAD_ROW // LANES
    anywhere = pl.BlockSpec(memory_space=pl.ANY)

    half = pltpu.VMEM((half_rows, LANES), BF16)
    mine, other = pl.pallas_call(
        pack_kernel,
        name="pack",
        out_shape=(half, half),
        in_specs=[anywhere] * 4,
        out_specs=vmem(2),
        scratch_shapes=[
            pltpu.VMEM((width, mix), BF16),
            pltpu.VMEM((width, mix), BF16),
            pltpu.SemaphoreType.DMA((4 + hidden // LANES,)),
        ],
        compiler_params=pltpu.CompilerParams(vmem_limit_bytes=PACK_VMEM_BYTES),
        cost_estimate=pl.CostEstimate(flops=5000000000, bytes_accessed=3000000, transcendentals=0),
    )(in_hbm(token_in[0].T), in_hbm(token_out[0]), in_hbm(chan_in[0]), in_hbm(chan_out[0]))

    def cross(x, distance):
        return lax.ppermute(x, "mod", [(i, i ^ distance) for i in range(owners)])

    got = {0: mine}
    for k in sorted(range(1, streams), key=lambda k: k != streams // 2):
        low = k & -k
        pairs = [(i, i ^ low) for i in range(streams)]
        got[k] = lax.ppermute(got[k ^ low], "stream", pairs)
    chips = owners // 2
    outgoing = pl.pallas_call(
        stem_kernel,
        name="stem",
        out_shape=(pltpu.VMEM((2, hit_rows + VETO_ROWS, channels), BF16),) * chips,
        in_specs=vmem(1) + [anywhere] * 3,
        out_specs=vmem(chips),
        scratch_shapes=[
            pltpu.VMEM((frames * columns // (2 * PATCH), 2 * PATCH * PATCH), BF16),
            pltpu.VMEM(stem_weight.shape, BF16),
            pltpu.VMEM((2 * PATCH * PATCH, 2 * channels), BF16),
            pltpu.VMEM(veto_weight.shape, F32),
            pltpu.VMEM((1, hits), jnp.int32),
            pltpu.VMEM((hits * width, channels), F32),
            pltpu.VMEM((frames, channels), F32),
            pltpu.SemaphoreType.DMA((3,)),
        ],
        compiler_params=pltpu.CompilerParams(vmem_limit_bytes=STEM_VMEM_BYTES),
        cost_estimate=pl.CostEstimate(flops=5_000_000_000, bytes_accessed=3_000_000, transcendentals=0),
    )(in_vmem(pixels[0]), in_hbm(stem_weight), in_hbm(veto_weight), in_hbm(hit_frames))
    received = [outgoing[0]] + [cross(outgoing[k], 2 * k) for k in range(1, chips)]
    bundle = pl.pallas_call(
        functools.partial(bundle_kernel, chips),
        name="bundle",
        out_shape=pltpu.VMEM((chips * (hit_rows + VETO_ROWS), LANES), BF16),
        in_specs=vmem(chips + 1),
        out_specs=vmem(1)[0],
        compiler_params=pltpu.CompilerParams(vmem_limit_bytes=PACK_VMEM_BYTES),
        cost_estimate=pl.CostEstimate(flops=1_000_000_000, bytes_accessed=1_000_000, transcendentals=0),
    )(*[in_vmem(x) for x in received[::-1]], in_vmem(got[1]))
    bundle = cross(bundle, 1)
    halves = [mine, other]
    for k in range(1, streams):
        halves += [got[k], cross(got[k], 1)]

    wides, veto = pl.pallas_call(
        functools.partial(prepare_kernel, width),
        name="prepare",
        out_shape=(
            pltpu.VMEM((hits_owned, PAD_ROW, owners * channels), BF16),
            jax.ShapeDtypeStruct((1, frames // owners), F32),
        ),
        in_specs=vmem(chips + 1),
        out_specs=tuple(vmem(2)),
        compiler_params=pltpu.CompilerParams(vmem_limit_bytes=PACK_VMEM_BYTES),
    )(*received[::-1], bundle)
    latents, scores = pl.pallas_call(
        functools.partial(encode_kernel, owners, streams, width, hidden),
        name="encode",
        out_shape=(
            jax.ShapeDtypeStruct((hits_owned, 1, channels), F32),
            jax.ShapeDtypeStruct((hits_owned, 1, class_weight.shape[1]), F32),
        ),
        in_specs=vmem(chips + 2)
        + [pl.BlockSpec(memory_space=pltpu.SMEM)]
        + vmem(3 + len(halves)),
        out_specs=tuple(vmem(2)),
        scratch_shapes=[
            pltpu.VMEM((hits_owned, 2, half_rows, LANES), BF16),
            pltpu.VMEM((8 * owners, channels), F32),
        ],
        compiler_params=pltpu.CompilerParams(vmem_limit_bytes=ENCODE_VMEM_BYTES),
    )(*received[::-1], bundle, wides, assign.reshape(hits), readout, latent_gain.reshape(1, channels), class_weight.T, *halves)
    return (veto, jnp.swapaxes(latents, 0, 1), jnp.swapaxes(scores, 0, 1))


def solution(mesh):
    in_specs = (
        P("stream", None, "mod", None),
        P(),
        P(),
        P("stream", None),
        P("stream", None, None),
        P("stream", None, None),
        P("stream", None, None),
        P("stream", None, None),
        P("stream", None, None),
        P(),
        P(),
        P(),
    )
    out_specs = (P("stream", "mod"), P("stream", "mod", None), P("stream", "mod", None))
    return jax.shard_map(local, mesh=mesh, in_specs=in_specs, out_specs=out_specs, check_vma=False)
```

```python
import functools
import math

import jax
import jax.numpy as jnp
from jax import lax
from jax.experimental import pallas as pl
from jax.experimental.pallas import tpu as pltpu
from jax.sharding import PartitionSpec as P

PATCH = 16
LANES = 128
GROUP = 16
VETO_ROWS = 16
PAD_ROW = 32
PACK_VMEM_BYTES = 16 * 1024 * 1024
STEM_VMEM_BYTES = 40 * 1024 * 1024
ENCODE_VMEM_BYTES = 32 * 1024 * 1024
F32 = jnp.float32
BF16 = jnp.bfloat16
GELU_A = math.sqrt(2.0 / math.pi)
GELU_B = GELU_A * 0.044715


def gelu(x):
    half = 0.5 * x
    return half + half * jnp.tanh(x * (GELU_A + GELU_B * (x * x)))


def double_gelu(x):
    x = x.astype(BF16)
    return x + x * jnp.tanh(x * (BF16(GELU_A) + BF16(GELU_B) * (x * x)))


def rms_norm(values):
    return values * lax.rsqrt(jnp.mean(values * values, axis=-1, keepdims=True) + 1e-06)


def dot(a, b):
    return jnp.dot(a, b, preferred_element_type=F32)


def dot_rows(a, b):
    return lax.dot_general(a, b, (((1,), (1,)), ((), ())), preferred_element_type=F32)


def split(x):
    top = x.astype(BF16)
    return top, (x - top.astype(F32)).astype(BF16)


def iota(shape, axis):
    return lax.broadcasted_iota(jnp.int32, shape, axis)


def pack_kernel(
    token_in, token_out, chan_in, chan_out, mine, other, token_in_rows, token_out_rows, sems
):
    core = lax.axis_index("mod") % 2
    channels, hidden = chan_in.shape
    width, mix = token_in.shape
    small = (
        pltpu.make_async_copy(token_in, token_in_rows, sems.at[0]),
        pltpu.make_async_copy(token_out, token_out_rows, sems.at[1]),
    )
    for c in small:
        c.start()

    def pack(first, second):
        large = [pltpu.make_async_copy(chan_out, second.at[pl.ds(0, hidden)], sems.at[2])]
        for j in range(hidden // LANES):
            large.append(
                pltpu.make_async_copy(
                    chan_in.at[:, pl.ds(j * LANES, LANES)], first.at[pl.ds(j * channels, channels)], sems.at[3 + j]
                )
            )
        for c in large:
            c.start()
        for c in small:
            c.wait()
        for source, ref in ((token_in_rows, first), (token_out_rows, second)):
            wide = source[...].astype(F32)
            wide = jnp.concatenate([wide, jnp.zeros((PAD_ROW - width, mix), F32)], axis=0).astype(BF16)
            for j in range(mix // LANES):
                ref[hidden + j * PAD_ROW : hidden + (j + 1) * PAD_ROW, :] = wide[:, j * LANES : (j + 1) * LANES]
        for c in large:
            c.wait()

    @pl.when(core == 0)
    def _():
        pack(mine, other)

    @pl.when(core == 1)
    def _():
        pack(other, mine)


def bundle_kernel(chips, *refs):
    features, out = refs[:chips], refs[-1]
    other = 1 - lax.axis_index("mod") % 2
    size = features[0].shape[1]
    for place, ref in enumerate(features):
        n = chips - 1 - place
        out[n * size : (n + 1) * size, :] = ref[other]


def turn(tiles, span):
    count = len(tiles)
    lane = iota(tiles[0].shape, 1)
    size = span * count // 2
    half = count // 2
    while half:
        low = (lane // size) % 2 == 0
        done = list(tiles)
        for i in range(count):
            if i // half % 2 == 0:
                a, b = tiles[i], tiles[i + half]
                done[i] = jnp.where(low, a, roll(b, size))
                done[i + half] = jnp.where(low, roll(a, LANES - size), b)
        tiles, half, size = done, half // 2, size // 2
    return tiles


def roll(x, shift):
    return jnp.concatenate([x[:, LANES - shift :], x[:, : LANES - shift]], axis=1)


def stem_kernel(
    images, weight, veto_weight, hit_frames, *refs
):
    out, (rows, small, wide, veto_rows, hit_row, chosen, totals, sems) = refs[:-8], refs[-8:]
    frames, _, columns = images.shape
    owners = 2 * len(out)
    hits = hit_frames.shape[1]
    owned = frames // owners
    hit_rows = out[0].shape[1] - VETO_ROWS
    channels = weight.shape[1]
    blocks = columns // LANES
    quads = LANES // (2 * PATCH)
    tokens = columns // PATCH
    side = [
        pltpu.make_async_copy(weight, small, sems.at[0]),
        pltpu.make_async_copy(veto_weight, veto_rows, sems.at[1]),
        pltpu.make_async_copy(hit_frames, hit_row, sems.at[2]),
    ]
    for c in side:
        c.start()
    size = GROUP * PATCH
    r, c = iota((size, size), 0), iota((size, size), 1)
    swap = (c == (r % GROUP) * PATCH + r // GROUP).astype(F32).astype(BF16)
    batch = math.gcd(frames // GROUP, 6)

    @pl.loop(0, frames // GROUP // batch)
    def _(i):
        for sub in range(batch):
            g = i * batch + sub
            block = images[pl.ds(pl.multiple_of(g * GROUP, GROUP), GROUP)].reshape(size, columns)
            turned = dot(swap, block).astype(BF16)
            for j in range(blocks):
                for p in range(0, PATCH, quads):
                    tiles = [
                        turned[q * GROUP : (q + 1) * GROUP, j * LANES : (j + 1) * LANES] for q in range(p, p + quads)
                    ]
                    for n, tile in enumerate(turn(tiles, 2 * PATCH)):
                        top = pl.multiple_of((n * blocks + j) * frames + g * GROUP, GROUP)
                        rows[pl.ds(top, GROUP), p * 2 * PATCH : p * 2 * PATCH + LANES] = tile

    for c in side:
        c.wait()
    zero = jnp.zeros((PATCH, channels), BF16)
    for p in range(PATCH):
        tile = small[p * PATCH : (p + 1) * PATCH, :]
        for a in range(2):
            top = (p * 2 + a) * PATCH
            for b in range(2):
                wide[top : top + PATCH, b * channels : (b + 1) * channels] = tile if a == b else zero
    pick = (iota((frames, hits), 0) == hit_row[...]).astype(F32).T.astype(BF16)
    sums = jnp.zeros((frames, channels), F32)
    spots = [(n, j) for n in range(quads) for j in range(blocks)]
    parts = [double_gelu(dot(rows[(n * blocks + j) * frames : (n * blocks + j + 1) * frames, :], wide[...])) for n, j in spots]
    for part in parts:
        sums = sums + part[:, :channels].astype(F32) + part[:, channels:].astype(F32)
    takens = [dot(pick, part.astype(BF16)) for part in parts]
    for (n, j), taken in zip(spots, takens):
        for k in range(2):
            chosen[pl.ds(j * 2 * quads + 2 * n + k, hits, stride=tokens), :] = taken[
                :, k * channels : (k + 1) * channels
            ]
    scale = jnp.broadcast_to(veto_rows[pl.ds(lax.axis_index("mod"), 1), :] / (2 * tokens), (VETO_ROWS, channels))
    row = iota((VETO_ROWS, owned), 0)
    totals[...] = sums
    scale_top, scale_low = split(scale)
    for k in range(owners // 2):
        for core in range(2):
            o = ((lax.axis_index("mod") // 2) ^ k) * 2 + core
            taken = 0.5 * chosen[pl.ds(pl.multiple_of(o * hit_rows, 8), hit_rows), :]
            out[k][core, 0:hit_rows, :] = taken.astype(BF16)
            top, low = split(totals[pl.ds(pl.multiple_of(o * owned, 8), owned), :])
            veto = dot_rows(scale_top, top) + (dot_rows(scale_top, low) + dot_rows(scale_low, top))
            high = veto.astype(BF16).astype(F32)
            both = jnp.where(row == 0, high, jnp.where(row == 1, veto - high, 0.0))
            both = jnp.concatenate([both, jnp.zeros((VETO_ROWS, LANES - owned), F32)], axis=1)
            out[k][core, hit_rows : hit_rows + VETO_ROWS, :] = both.astype(BF16)


def prepare_kernel(width, *refs):
    chips = len(refs) - 3
    received, bundle, wides, veto = refs[:chips][::-1], refs[chips], refs[chips + 1], refs[chips + 2]
    core = lax.axis_index("mod") % 2
    hits = wides.shape[0]
    channels = received[0].shape[2]
    hit_rows = hits * width
    block = hit_rows + VETO_ROWS
    gap = jnp.zeros((hits, PAD_ROW - width, channels), F32)
    for n, ref in enumerate(received):
        parts = (ref[core, 0:hit_rows, :], bundle[n * block : n * block + hit_rows, :])
        for c, part in enumerate(parts):
            normed = rms_norm(part.astype(F32).reshape(hits, width, channels))
            r = 2 * n + c
            wides[:, :, r * channels : (r + 1) * channels] = jnp.concatenate([normed, gap], axis=1).astype(BF16)
    tails = [ref[core, hit_rows:block, :] for ref in received]
    tails += [bundle[n * block + hit_rows : (n + 1) * block, :] for n in range(chips)]
    terms = sum(tail.astype(F32) for tail in tails)
    veto[...] = jnp.sum(terms, axis=0, keepdims=True)[:, : veto.shape[1]]


def encode_kernel(owners, streams, width, hidden, *refs):
    chips = owners // 2
    received, bundle, wides, refs = refs[:chips][::-1], refs[chips], refs[chips + 1], refs[chips + 2 :]
    targets, readout, gain, class_weight = refs[:4]
    halves = refs[4 : 4 + 2 * streams]
    latents, scores, table, pools = refs[4 + 2 * streams :]
    channels = received[0].shape[2]
    hits = latents.shape[0]
    hit_rows = hits * width
    block = hit_rows + VETO_ROWS
    here = lax.axis_index("stream")
    own = lax.axis_index("mod")
    core = own % 2

    for slot in range(hits):
        wanted = targets[own * hits + slot] ^ here
        for k in range(streams):

            @pl.when(wanted == k)
            def _():
                table[slot, core] = halves[2 * k][...]
                table[slot, 1 - core] = halves[2 * k + 1][...]

    pools[...] = jnp.zeros_like(pools)

    extra = table.shape[2] - hidden
    blocks = extra // PAD_ROW

    def widen(slot, half):
        return jnp.concatenate(
            [table[slot, half, hidden + j * PAD_ROW : hidden + (j + 1) * PAD_ROW, :] for j in range(blocks)], axis=1
        )

    def mix_in(slot):
        token_in = widen(slot, 0).astype(F32).T.astype(BF16)
        return double_gelu(dot(token_in, wides[slot]))

    def mix_out(slot, x, mixed):
        back = 0.5 * dot(widen(slot, 1), mixed)
        after = jnp.concatenate(
            [x[r] + back[:width, r * channels : (r + 1) * channels] for r in range(owners)], axis=0
        )
        return after.astype(BF16).astype(F32)

    def channel_in(slot, after):
        chan_in = jnp.concatenate(
            [table[slot, 0, j * channels : (j + 1) * channels, :] for j in range(hidden // channels)], axis=1
        )
        return double_gelu(dot(rms_norm(after).astype(BF16), chan_in))

    def channel_out(slot, after, inner):
        last = after + 0.5 * dot(inner, table[slot, 1, 0:hidden, :])
        pool = jnp.sum(last.reshape(owners, width, channels), axis=1) * (1.0 / width)
        pools[pl.ds(pl.multiple_of(slot * owners, owners), owners), :] = pool

    group = hits if owners <= 8 else 2

    @pl.loop(0, hits // group)
    def _(i):
        first = i * group
        start = pl.multiple_of(first * width, 16)
        every = []
        for n, ref in enumerate(received):
            every.append(ref[core, pl.ds(start, group * width), :].astype(F32))
            every.append(bundle[pl.ds(n * block + start, group * width), :].astype(F32))
        every = jnp.stack(every)
        slots = [first + a for a in range(group)]
        x = [every[:, a * width : (a + 1) * width] for a in range(group)]
        mixed = [mix_in(n) for n in slots]
        after = [mix_out(n, v, m) for n, v, m in zip(slots, x, mixed)]
        inner = [channel_in(n, v) for n, v in zip(slots, after)]
        for n, v, m in zip(slots, after, inner):
            channel_out(n, v, m)

    pooled = jnp.concatenate(
        [pools[pl.ds(r, 8, stride=owners), :].astype(BF16) for r in range(owners)], axis=1
    )
    modules = [((own // 2) ^ (r // 2)) * 2 + (core if r % 2 == 0 else 1 - core) for r in range(owners)]
    weights = [readout[pl.ds(pl.multiple_of(m * channels, channels), channels), :] for m in modules]
    latent = rms_norm(dot(pooled, jnp.concatenate(weights, axis=0))) * gain[...]
    latents[:, 0, :] = latent[:hits]
    scores[:, 0, :] = lax.dot_general(
        latent,
        class_weight[...],
        (((1,), (1,)), ((), ())),
        preferred_element_type=F32,
        precision=lax.Precision.HIGHEST,
    )[:hits]


def vmem(count):
    return [pl.BlockSpec(memory_space=pltpu.VMEM)] * count


def in_vmem(x):
    return pltpu.with_memory_space_constraint(x, pltpu.VMEM)


def in_hbm(x):
    return pltpu.with_memory_space_constraint(x, pltpu.HBM)


def local(
    pixels,
    stem_weight,
    veto_weight,
    hit_frames,
    assign,
    token_in,
    token_out,
    chan_in,
    chan_out,
    readout,
    latent_gain,
    class_weight,
):
    owners = lax.axis_size("mod")
    streams = lax.axis_size("stream")
    _, frames, height, columns = pixels.shape
    channels = stem_weight.shape[1]
    mix, width = token_in.shape[1:]
    hidden = chan_in.shape[2]
    hits = hit_frames.shape[1]
    hits_owned = hits // owners
    hit_rows = hits_owned * width
    half_rows = hidden + mix * PAD_ROW // LANES
    anywhere = pl.BlockSpec(memory_space=pl.ANY)

    half = pltpu.VMEM((half_rows, LANES), BF16)
    mine, other = pl.pallas_call(
        pack_kernel,
        name="pack",
        out_shape=(half, half),
        in_specs=[anywhere] * 4,
        out_specs=vmem(2),
        scratch_shapes=[
            pltpu.VMEM((width, mix), BF16),
            pltpu.VMEM((width, mix), BF16),
            pltpu.SemaphoreType.DMA((4 + hidden // LANES,)),
        ],
        compiler_params=pltpu.CompilerParams(vmem_limit_bytes=PACK_VMEM_BYTES),
        cost_estimate=pl.CostEstimate(flops=5000000000, bytes_accessed=3000000, transcendentals=0),
    )(in_hbm(token_in[0].T), in_hbm(token_out[0]), in_hbm(chan_in[0]), in_hbm(chan_out[0]))

    def cross(x, distance):
        return lax.ppermute(x, "mod", [(i, i ^ distance) for i in range(owners)])

    got = {0: mine}
    for k in sorted(range(1, streams), key=lambda k: k != streams // 2):
        low = k & -k
        pairs = [(i, i ^ low) for i in range(streams)]
        got[k] = lax.ppermute(got[k ^ low], "stream", pairs)
    chips = owners // 2
    outgoing = pl.pallas_call(
        stem_kernel,
        name="stem",
        out_shape=(pltpu.VMEM((2, hit_rows + VETO_ROWS, channels), BF16),) * chips,
        in_specs=vmem(1) + [anywhere] * 3,
        out_specs=vmem(chips),
        scratch_shapes=[
            pltpu.VMEM((frames * columns // (2 * PATCH), 2 * PATCH * PATCH), BF16),
            pltpu.VMEM(stem_weight.shape, BF16),
            pltpu.VMEM((2 * PATCH * PATCH, 2 * channels), BF16),
            pltpu.VMEM(veto_weight.shape, F32),
            pltpu.VMEM((1, hits), jnp.int32),
            pltpu.VMEM((hits * width, channels), F32),
            pltpu.VMEM((frames, channels), F32),
            pltpu.SemaphoreType.DMA((3,)),
        ],
        compiler_params=pltpu.CompilerParams(vmem_limit_bytes=STEM_VMEM_BYTES),
        cost_estimate=pl.CostEstimate(flops=5_000_000_000, bytes_accessed=3_000_000, transcendentals=0),
    )(in_vmem(pixels[0]), in_hbm(stem_weight), in_hbm(veto_weight), in_hbm(hit_frames))
    received = [outgoing[0]] + [cross(outgoing[k], 2 * k) for k in range(1, chips)]
    bundle = pl.pallas_call(
        functools.partial(bundle_kernel, chips),
        name="bundle",
        out_shape=pltpu.VMEM((chips * (hit_rows + VETO_ROWS), LANES), BF16),
        in_specs=vmem(chips + 1),
        out_specs=vmem(1)[0],
        compiler_params=pltpu.CompilerParams(vmem_limit_bytes=PACK_VMEM_BYTES),
        cost_estimate=pl.CostEstimate(flops=1_000_000_000, bytes_accessed=1_000_000, transcendentals=0),
    )(*[in_vmem(x) for x in received[::-1]], in_vmem(got[1]))
    bundle = cross(bundle, 1)
    halves = [mine, other]
    for k in range(1, streams):
        halves += [got[k], cross(got[k], 1)]

    wides, veto = pl.pallas_call(
        functools.partial(prepare_kernel, width),
        name="prepare",
        out_shape=(
            pltpu.VMEM((hits_owned, PAD_ROW, owners * channels), BF16),
            jax.ShapeDtypeStruct((1, frames // owners), F32),
        ),
        in_specs=vmem(chips + 1),
        out_specs=tuple(vmem(2)),
        compiler_params=pltpu.CompilerParams(vmem_limit_bytes=PACK_VMEM_BYTES),
    )(*received[::-1], bundle)
    latents, scores = pl.pallas_call(
        functools.partial(encode_kernel, owners, streams, width, hidden),
        name="encode",
        out_shape=(
            jax.ShapeDtypeStruct((hits_owned, 1, channels), F32),
            jax.ShapeDtypeStruct((hits_owned, 1, class_weight.shape[1]), F32),
        ),
        in_specs=vmem(chips + 2)
        + [pl.BlockSpec(memory_space=pltpu.SMEM)]
        + vmem(3 + len(halves)),
        out_specs=tuple(vmem(2)),
        scratch_shapes=[
            pltpu.VMEM((hits_owned, 2, half_rows, LANES), BF16),
            pltpu.VMEM((8 * owners, channels), F32),
        ],
        compiler_params=pltpu.CompilerParams(vmem_limit_bytes=ENCODE_VMEM_BYTES),
    )(*received[::-1], bundle, wides, assign.reshape(hits), readout, latent_gain.reshape(1, channels), class_weight.T, *halves)
    return (veto, jnp.swapaxes(latents, 0, 1), jnp.swapaxes(scores, 0, 1))


def solution(mesh):
    in_specs = (
        P("stream", None, "mod", None),
        P(),
        P(),
        P("stream", None),
        P("stream", None, None),
        P("stream", None, None),
        P("stream", None, None),
        P("stream", None, None),
        P("stream", None, None),
        P(),
        P(),
        P(),
    )
    out_specs = (P("stream", "mod"), P("stream", "mod", None), P("stream", "mod", None))
    return jax.shard_map(local, mesh=mesh, in_specs=in_specs, out_specs=out_specs, check_vma=False)
```
